32 devices in a mesh: energy: 2 (over x), slab: 8 (over z, y), row: 2 (over core).
Axes of the slice: x: 2, y: 2, z: 4, core: 2. Of those that a mesh axis runs over, the one named last changes fastest.
Arguments:
- green_blocks: bfloat16 [2, 12288, 768], P(None, ('energy', 'slab', 'row')), parts along dimension 1, may hold values from -3 to 3
- coupling: bfloat16 [2, 1024, 128], P(None, 'slab'), may hold values from -2 to 2
- source: bfloat16 [2, 12288, 128], P(None, ('energy', 'slab', 'row')), parts along dimension 1, may hold values from -6 to 6
- interior_count: int32 [8], P('slab'), may hold values from 256 to 512, as said below
Outputs:
- solution: float32 [2, 12288, 128], P(None, ('energy', 'slab', 'row')), parts along dimension 1
The draws below stay inside these ranges and needn't reach their ends.
There are 2 independent parts, one for each index of `energy`. The reference program is written for one: setup_inputs(seed, part) draws one part's arguments, and reference() takes and returns one part's arrays. A program takes and returns all parts, laid end to end along the dimension named above; an argument that names none is the same for every part. Nothing has to cross between parts.
Inputs may be any that keep to these rules, and one draw needn't show every extreme that they name: `interior_count`: some slab has exactly 512 live interior orbitals.
All inputs are finite; a program needn't handle non-finite values.
Results may differ from the reference program's by a relative error of at most 0.0095.
Values may be sent and summed in bfloat16 or wider, within the bound.
A program may use at most 128 MiB of HBM per device.

```python
import math
import jax
import jax.numpy as jnp
from jax import lax

ORB = 768
IFC = 128
NRHS = 128
WIRE_SLABS = 8


def draw_green_blocks(key, part):
    random_keys = jax.random.split(jax.random.fold_in(key, 101), 9)
    noise = jax.random.truncated_normal(random_keys[0], -4.0, 4.0, (2, WIRE_SLABS, ORB, ORB)) * (0.3 / math.sqrt(ORB))
    position = jnp.arange(ORB)
    corner = (position[:, None] >= ORB - IFC) & (position[None, :] < IFC)
    noise = noise * jnp.where(corner, 0.3, 1.0)
    diag_real = jax.random.uniform(random_keys[1], (WIRE_SLABS, ORB), minval=0.6, maxval=1.4)
    diag_imag = jax.random.uniform(random_keys[2], (WIRE_SLABS, ORB), minval=-0.4, maxval=0.4)
    unit_orb = jnp.eye(ORB, dtype=jnp.float32)
    result = noise + jnp.stack([diag_real, diag_imag])[:, :, :, None] * unit_orb
    slow_share = 0.5
    slow = jax.random.uniform(random_keys[3], (IFC,)) < slow_share
    gradual_rate = jax.random.uniform(random_keys[4], (WIRE_SLABS, IFC), minval=0.93, maxval=0.97)
    sudden_spike = jax.random.uniform(random_keys[5], (WIRE_SLABS, 1)) < 0.06
    gradual_rate = gradual_rate * jnp.where(sudden_spike, 0.6, 1.0)
    fast_rate = jnp.exp(jax.random.uniform(random_keys[6], (WIRE_SLABS, IFC), minval=math.log(0.15), maxval=math.log(0.6)))
    rate = jnp.where(slow[None, :], gradual_rate, fast_rate)
    unit_ifc = jnp.eye(IFC, dtype=jnp.float32)
    phase_lf = jax.random.uniform(random_keys[7], (WIRE_SLABS, IFC), minval=-math.pi, maxval=math.pi)
    phase_fl = jax.random.uniform(random_keys[8], (WIRE_SLABS, IFC), minval=-math.pi, maxval=math.pi)
    link_lf = jnp.stack([rate * jnp.cos(phase_lf), rate * jnp.sin(phase_lf)])[:, :, :, None] * unit_ifc
    link_fl = jnp.stack([rate * jnp.cos(phase_fl), rate * jnp.sin(phase_fl)])[:, :, :, None] * unit_ifc
    result = result + jnp.pad(link_lf, ((0, 0), (0, 0), (ORB - IFC, 0), (0, ORB - IFC)))
    result = result + jnp.pad(link_fl, ((0, 0), (0, 0), (0, ORB - IFC), (ORB - IFC, 0)))
    return result.reshape(2, WIRE_SLABS * ORB, ORB).astype(jnp.bfloat16)


def draw_coupling(key, part):
    random_keys = jax.random.split(jax.random.fold_in(key, 202), 2)
    phase = jax.random.uniform(random_keys[0], (WIRE_SLABS, IFC), minval=-math.pi, maxval=math.pi)
    spread = 0.15
    noise = jax.random.truncated_normal(random_keys[1], -4.0, 4.0, (2, WIRE_SLABS, IFC, IFC)) * (spread / math.sqrt(IFC))
    unit_ifc = jnp.eye(IFC, dtype=jnp.float32)
    result = noise + jnp.stack([jnp.cos(phase), jnp.sin(phase)])[:, :, :, None] * unit_ifc
    return result.reshape(2, WIRE_SLABS * IFC, IFC).astype(jnp.bfloat16)


def draw_interior_count(key, part):
    random_keys = jax.random.split(jax.random.fold_in(key, 303), 2)
    minimum_level = (ORB - 2 * IFC) // 2
    highest = ORB - 2 * IFC
    counts = jax.random.randint(random_keys[0], (WIRE_SLABS,), minimum_level, highest + 1)
    chosen = jax.random.randint(random_keys[1], (), 0, WIRE_SLABS)
    return counts.at[chosen].set(highest).astype(jnp.int32)


def steps_of(stream_key, shape, pieces, smallest, high):
    def one(dim, shards_of):
        draws = jax.random.uniform(jax.random.fold_in(jax.random.fold_in(stream_key, 6), dim), (shards_of,), jnp.float32, smallest / len(pieces), high / len(pieces))
        return jnp.repeat(jnp.exp(draws), shape[dim] // shards_of).reshape((-1,) + (1,) * (len(shape) - dim - 1))

    level = one(*pieces[0])
    for cut in pieces[1:]:
        level = level * one(*cut)
    return level


def bell_draw(key, shape, scale, limit, cuts=(), kind=jnp.bfloat16):
    factor_of = steps_of(key, shape, cuts, -0.22, 0.18) if cuts else 1.0
    entries = jax.random.normal(key, shape, jnp.float32) * scale * factor_of
    return jnp.minimum(jnp.maximum(entries, -limit), limit).astype(kind)


def setup_inputs(seed: int = 0, part: int = 0) -> dict:
    key_list = jax.random.split(jax.random.key(seed), 5)
    part_keys = jax.random.split(jax.random.fold_in(key_list[4], part), 5)
    green_blocks = draw_green_blocks(jax.random.fold_in(jax.random.fold_in(key_list[4], part), 71), part)
    coupling = draw_coupling(jax.random.fold_in(key_list[4], 71), part)
    source = bell_draw(part_keys[2], (2, WIRE_SLABS * ORB, NRHS), 1.0, 6.0, ((1, 16),))
    interior_count = draw_interior_count(jax.random.fold_in(key_list[4], 71), part)
    return {"green_blocks": green_blocks, "coupling": coupling, "source": source, "interior_count": interior_count}


def multiply(matrix, operand):
    return jnp.matmul(matrix, operand, precision=lax.Precision.HIGHEST)


def complex_product(matrix, operand):
    real_part = multiply(matrix[0], operand[0]) - multiply(matrix[1], operand[1])
    imag_part = multiply(matrix[0], operand[1]) + multiply(matrix[1], operand[0])
    return jnp.stack([real_part, imag_part])


def adjoint(matrix):
    return jnp.stack([jnp.swapaxes(matrix[0], -1, -2), -jnp.swapaxes(matrix[1], -1, -2)])


def sweep_step(state, element):
    mapping, term = element
    return complex_product(mapping, state) + term, state


def reference(green_blocks, coupling, source, interior_count):
    green = green_blocks.astype(jnp.float32).reshape(2, WIRE_SLABS, ORB, ORB)
    slab_coupling = coupling.astype(jnp.float32).reshape(2, WIRE_SLABS, IFC, IFC)
    inject = source.astype(jnp.float32).reshape(2, WIRE_SLABS, ORB, NRHS)
    orbital = jnp.arange(ORB, dtype=jnp.int32)
    live = ((orbital[None, :] < IFC + interior_count[:, None]) | (orbital[None, :] >= ORB - IFC)).astype(jnp.float32)
    inject = inject * live[None, :, :, None]
    direct = complex_product(green, inject)
    edge_first = direct[:, :, :IFC]
    edge_last = direct[:, :, ORB - IFC:]
    zero_block = jnp.zeros((2, 1, IFC, IFC), jnp.float32)
    couple_next = jnp.concatenate([slab_coupling[:, :-1], zero_block], axis=1)
    couple_prev = jnp.concatenate([zero_block, slab_coupling[:, :-1]], axis=1)
    first_next = jnp.concatenate([edge_first[:, 1:], jnp.zeros((2, 1, IFC, NRHS), jnp.float32)], axis=1)
    green_ff = green[:, :, :IFC, :IFC]
    green_fl = green[:, :, :IFC, ORB - IFC:]
    green_lf = green[:, :, ORB - IFC:, :IFC]
    green_ll = green[:, :, ORB - IFC:, ORB - IFC:]
    forward_map = complex_product(green_lf, adjoint(couple_prev))
    forward_term = edge_last + complex_product(green_ll, complex_product(couple_next, first_next))
    start = jnp.zeros((2, IFC, NRHS), jnp.float32)
    _, preceding_slab = lax.scan(sweep_step, start, (jnp.moveaxis(forward_map, 1, 0), jnp.moveaxis(forward_term, 1, 0)))
    preceding_slab = jnp.moveaxis(preceding_slab, 0, 1)
    lower = complex_product(adjoint(couple_prev), preceding_slab)
    reverse_mapping = complex_product(green_fl, couple_next)
    backward_term = edge_first + complex_product(green_ff, lower)
    _, after = lax.scan(sweep_step, start, (jnp.moveaxis(reverse_mapping, 1, 0), jnp.moveaxis(backward_term, 1, 0)), reverse=True)
    after = jnp.moveaxis(after, 0, 1)
    upper = complex_product(couple_next, after)
    lower_round = lax.optimization_barrier(lower.astype(jnp.bfloat16)).astype(jnp.float32)
    upper_round = lax.optimization_barrier(upper.astype(jnp.bfloat16)).astype(jnp.float32)
    result = direct + complex_product(green[:, :, :, :IFC], lower_round) + complex_product(green[:, :, :, ORB - IFC:], upper_round)
    result = result * live[None, :, :, None]
    return result.reshape(2, WIRE_SLABS * ORB, NRHS)
```

```python
import functools

import jax
import jax.numpy as jnp
from jax import lax
from jax.experimental import pallas as pl
from jax.experimental.pallas import tpu as pltpu
from jax.sharding import PartitionSpec as P

F32 = jnp.float32
BF16 = jnp.bfloat16

SOURCE, COUPLE, EDGE, MAP_A, TERM_A, BACK_B, CROSS_B, FIRST_B, STATE, LOWER, AFTER, UPPER = range(12)
(S_SOURCE, S_COUPLE, S_EDGE, S_0, S_1, S_2, S_3, S_LOWER, S_UPPER) = range(9)


def dot(a, b):
    return jnp.dot(a, b, preferred_element_type=F32)


def embed(real, imag):
    return jnp.concatenate(
        [jnp.concatenate([real, -imag], axis=1), jnp.concatenate([imag, real], axis=1)], axis=0
    )


def halves(x):
    high = x.astype(BF16)
    return high, (x - high.astype(F32)).astype(BF16)


def wide_map(x):
    w = x.shape[0] // 2
    high, low = halves(x)
    return embed(high[:w], high[w:]), embed(low[:w], low[w:])


def apply_exact(matrix, x):
    c = x.shape[1]
    y = dot(matrix, jnp.concatenate(halves(x), axis=1))
    return y[:, :c] + y[:, c:]


def apply_wide(matrix, x):
    c = x.shape[1]
    high, low = halves(x)
    y = dot(matrix[0], jnp.concatenate([high, low], axis=1))
    return y[:, :c] + (y[:, c:] + dot(matrix[1], high))


def kernel(
    count, green_hbm, couple_hbm, source_hbm, interior_ref, out_ref,
    green, couple, source, source_in, couple_in, edge_in, map_a, term_a, back_b, cross_b, first_b,
    state, lower, after, upper, edge_out, out_0, out_1, out_2, low_out, up_out,
    copy_sem, send_sem, recv_sem,
):
    rows, width = green.shape[1], green.shape[2]
    w = couple.shape[1]
    cols = source.shape[2]
    s = lax.axis_index("slab")
    r = lax.axis_index("row")
    odd = lax.rem(s, 2)
    pair = s // 2
    pairs = count // 2

    loads = [
        pltpu.make_async_copy(source_hbm, source, copy_sem.at[0]),
        pltpu.make_async_copy(green_hbm, green, copy_sem.at[1]),
        pltpu.make_async_copy(couple_hbm, couple, copy_sem.at[2]),
    ]
    for load in loads:
        load.start()

    buffers = [source_in, couple_in, edge_in, map_a, term_a, back_b, cross_b, first_b, state, lower, after, upper]

    def push(src, slot, out_slot, slab, row):
        copy = pltpu.make_async_remote_copy(
            src_ref=src, dst_ref=buffers[slot], send_sem=send_sem.at[out_slot], recv_sem=recv_sem.at[slot],
            device_id={"slab": slab, "row": row}, device_id_type=pl.DeviceIdType.MESH,
        )
        copy.start()
        return copy

    def arrived(slot):
        pltpu.make_async_remote_copy(
            src_ref=buffers[slot], dst_ref=buffers[slot], send_sem=send_sem.at[0], recv_sem=recv_sem.at[slot],
            device_id={"slab": s, "row": 1 - r}, device_id_type=pl.DeviceIdType.MESH,
        ).wait_recv()

    def sent(src, out_slot):
        pltpu.make_async_remote_copy(
            src_ref=src, dst_ref=src, send_sem=send_sem.at[out_slot], recv_sem=recv_sem.at[0],
            device_id={"slab": s, "row": 1 - r}, device_id_type=pl.DeviceIdType.MESH,
        ).wait_send()

    barrier = pltpu.get_barrier_semaphore()
    leader = jnp.logical_or(jnp.logical_and(odd == 0, r == 0), jnp.logical_and(odd == 1, r == 1))
    side = jnp.where(r == 1, s + 1, s - 1)
    partners = [
        (s, 1 - r, None),
        (s - 1, r, s > 0),
        (s + 1, r, s < count - 1),
        (side, 1 - r, jnp.logical_and(side >= 0, side < count)),
        (s - 2, r, jnp.logical_and(leader, s >= 2)),
        (s + 2, r, jnp.logical_and(leader, s < count - 2)),
    ]
    expected = 1
    for slab, row, there in partners:
        def greet(slab=slab, row=row):
            pl.semaphore_signal(
                barrier, inc=1, device_id={"slab": slab, "row": row}, device_id_type=pl.DeviceIdType.MESH
            )
        if there is None:
            greet()
        else:
            pl.when(there)(greet)
            expected = expected + there.astype(jnp.int32)
    pl.semaphore_wait(barrier, expected)

    push(source_hbm, SOURCE, S_SOURCE, s, 1 - r)

    @pl.when(s < count - 1)
    def _():
        push(couple_hbm, COUPLE, S_COUPLE, s + 1, r)

    interior = interior_ref[0]

    def injected(ref, half):
        orbital = half * rows + lax.broadcasted_iota(jnp.int32, (rows, cols), 0)
        live = jnp.logical_or(orbital < w + interior, orbital >= width - w).astype(F32)
        return jnp.concatenate(
            [(ref[0].astype(F32) * live).astype(BF16), (ref[1].astype(F32) * live).astype(BF16)], axis=1
        )

    def add_product(x, columns, first):
        by_real = dot(green[0, :, columns], x)
        by_imag = dot(green[1, :, columns], x)
        real = by_real[:, :cols] - by_imag[:, cols:]
        imag = by_real[:, cols:] + by_imag[:, :cols]
        if first:
            out_ref[0], out_ref[1] = real, imag
        else:
            out_ref[0] += real
            out_ref[1] += imag

    loads[0].wait()
    loads[1].wait()
    add_product(injected(source, r), pl.ds(pl.multiple_of(r * rows, w), rows), True)
    arrived(SOURCE)
    add_product(injected(source_in, 1 - r), pl.ds(pl.multiple_of((1 - r) * rows, w), rows), False)

    loads[2].wait()
    head, tail = slice(0, w), slice(width - w, width)
    has_next = (s < count - 1).astype(F32)

    def next_coupling():
        return (couple[...].astype(F32) * has_next).astype(BF16).reshape(2 * w, w)

    def previous_coupling():
        @pl.when(s > 0)
        def _():
            arrived(COUPLE)

        @pl.when(s == 0)
        def _():
            couple_in[...] = jnp.zeros_like(couple_in)

    def previous_adjoint():
        return (
            couple_in[0].astype(F32).T.astype(BF16),
            (-couple_in[1].astype(F32).T).astype(BF16),
        )

    def block(first_row, columns):
        return embed(
            green[0, first_row:first_row + w, columns], green[1, first_row:first_row + w, columns]
        )

    def surface(first_row):
        return jnp.concatenate(
            [out_ref[0, first_row:first_row + w, :], out_ref[1, first_row:first_row + w, :]], axis=0
        )

    def pairwise(ref):
        return jnp.concatenate([ref[:w], ref[w:]], axis=1)

    def no_state(ref, there, slot):
        @pl.when(there)
        def _():
            arrived(slot)

        @pl.when(jnp.logical_not(there))
        def _():
            ref[...] = jnp.zeros_like(ref)

    def row_zero(even):
        first = surface(0)
        edge_out[...] = first.astype(BF16)

        @pl.when(s > 0)
        def _():
            push(edge_out, EDGE, S_EDGE, s - 1, 1)

        if not even:
            out_0[...] = first
            push(out_0, FIRST_B, S_0, s - 1, 0)
        couple_now = next_coupling()
        back = dot(block(0, tail), couple_now)
        if not even:
            out_1[...] = back
            push(out_1, BACK_B, S_1, s - 1, 0)
        previous_coupling()
        adj_real, adj_imag = previous_adjoint()
        adjoint = embed(adj_real, adj_imag)
        cross = dot(block(0, head), jnp.concatenate([adj_real, adj_imag], axis=0))
        if not even:
            out_2[...] = cross
            push(out_2, CROSS_B, S_2, s - 1, 0)
            couple_map = embed(couple_now[:w], couple_now[w:])
            arrived(STATE)
        else:
            couple_map = embed(couple_now[:w], couple_now[w:])
            arrived(BACK_B)
            back_own = wide_map(back)
            back_two = wide_map(apply_wide(back_own, back_b[...]))
            back_far = wide_map(back_b[...])
            arrived(CROSS_B)
            arrived(MAP_A)
            cross_far = wide_map(cross_b[...])
            cross_two_f = apply_wide(cross_far, map_a[...])
            cross_two = wide_map(cross_two_f)
            cross_all = wide_map(cross + apply_wide(back_own, cross_two_f))
            arrived(FIRST_B)
            arrived(TERM_A)
            term_b = first_b[...] + apply_wide(cross_far, term_a[...])
            term = first + apply_wide(back_own, term_b)
            no_state(state, pair > 0, STATE)
            before = state[...]
            term = term + apply_wide(cross_all, before)
            no_state(after, pair < pairs - 1, AFTER)
            follow = after[...]
            out_0[...] = term + apply_wide(back_two, follow)

            @pl.when(pair > 0)
            def _():
                push(out_0, AFTER, S_0, s - 2, 0)
                push(out_0, AFTER, S_1, s - 1, 0)

            after_own = term_b + apply_wide(cross_two, before) + apply_wide(back_far, follow)
        low_out[...] = apply_exact(adjoint, state[...]).astype(BF16)
        push(low_out, LOWER, S_LOWER, s, 1)
        if even:
            up_out[...] = apply_exact(couple_map, after_own).astype(BF16)
            push(up_out, UPPER, S_UPPER, s, 1)
            add_product(pairwise(low_out), head, False)
            add_product(pairwise(up_out), tail, False)
        else:
            add_product(pairwise(low_out), head, False)
            no_state(after, pair < pairs - 1, AFTER)
            up_out[...] = apply_exact(couple_map, after[...]).astype(BF16)
            push(up_out, UPPER, S_UPPER, s, 1)
            add_product(pairwise(up_out), tail, False)
        sent(low_out, S_LOWER)
        sent(up_out, S_UPPER)

        @pl.when(s > 0)
        def _():
            sent(edge_out, S_EDGE)

        if even:
            @pl.when(pair > 0)
            def _():
                sent(out_0, S_0)
                sent(out_0, S_1)
        else:
            sent(out_0, S_0)
            sent(out_1, S_1)
            sent(out_2, S_2)

    def row_one(even):
        last = surface(rows - w)
        previous_coupling()
        adj_real, adj_imag = previous_adjoint()
        forward = dot(block(rows - w, head), jnp.concatenate([adj_real, adj_imag], axis=0))
        if even:
            out_0[...] = forward
            push(out_0, MAP_A, S_0, s, 0)
            push(out_0, MAP_A, S_1, s + 1, 1)
        else:
            own = wide_map(forward)
        turned = wide_map(dot(block(rows - w, tail), next_coupling()))
        if even:
            arrived(EDGE)
            edge = edge_in[...]
        else:
            no_state(edge_in, s < count - 1, EDGE)
            edge = edge_in[...]
        term = last + dot(turned[0], edge) + dot(turned[1], edge)
        if even:
            out_1[...] = term
            push(out_1, TERM_A, S_2, s + 1, 1)
            push(out_1, TERM_A, S_3, s, 0)
        else:
            arrived(MAP_A)
            both = wide_map(apply_wide(own, map_a[...]))
            near = wide_map(map_a[...])
            arrived(TERM_A)
            total = term + apply_wide(own, term_a[...])
            no_state(state, pair > 0, STATE)
            before = state[...]

            @pl.when(pair < pairs - 1)
            def _():
                out_0[...] = total + apply_wide(both, before)

                @pl.when(pair == pairs - 2)
                def _():
                    push(out_0, STATE, S_0, s + 1, 0)
                    push(out_0, STATE, S_1, s + 2, 1)

                @pl.when(pair < pairs - 2)
                def _():
                    push(out_0, STATE, S_1, s + 2, 1)
                    push(out_0, STATE, S_0, s + 1, 0)

            out_1[...] = term_a[...] + apply_wide(near, before)
            push(out_1, STATE, S_2, s, 0)
        arrived(LOWER)
        add_product(pairwise(lower), head, False)
        arrived(UPPER)
        add_product(pairwise(upper), tail, False)
        if even:
            sent(out_0, S_0)
            sent(out_0, S_1)
            sent(out_1, S_2)
            sent(out_1, S_3)
        else:
            @pl.when(pair < pairs - 1)
            def _():
                sent(out_0, S_0)
                sent(out_0, S_1)

            sent(out_1, S_2)

    for row, role in ((0, row_zero), (1, row_one)):
        for parity in (0, 1):
            @pl.when(jnp.logical_and(r == row, odd == parity))
            def _(role=role, parity=parity):
                role(parity == 0)

    sent(source_hbm, S_SOURCE)

    @pl.when(s < count - 1)
    def _():
        sent(couple_hbm, S_COUPLE)


def body(green_blocks, coupling, source, interior_count):
    rows, width = green_blocks.shape[1:]
    w = coupling.shape[1]
    cols = source.shape[2]
    block = pltpu.VMEM((2 * w, cols), F32)
    small = pltpu.VMEM((2 * w, cols), BF16)
    square = pltpu.VMEM((2 * w, w), F32)
    result = pl.pallas_call(
        functools.partial(kernel, lax.axis_size("slab")),
        out_shape=jax.ShapeDtypeStruct((2, rows, cols), F32),
        in_specs=[pl.BlockSpec(memory_space=pl.ANY)] * 3 + [pl.BlockSpec(memory_space=pltpu.SMEM)],
        out_specs=pl.BlockSpec(memory_space=pltpu.VMEM),
        scratch_shapes=[
            pltpu.VMEM(green_blocks.shape, BF16),
            pltpu.VMEM(coupling.shape, BF16),
            pltpu.VMEM(source.shape, BF16),
            pltpu.VMEM(source.shape, BF16),
            pltpu.VMEM(coupling.shape, BF16),
            small,
            square,
            block,
            square,
            square,
            block,
            block,
            small,
            block,
            small,
            small,
            block,
            block,
            square,
            small,
            small,
            pltpu.SemaphoreType.DMA((3,)),
            pltpu.SemaphoreType.DMA((9,)),
            pltpu.SemaphoreType.DMA((12,)),
        ],
        compiler_params=pltpu.CompilerParams(
            collective_id=0, has_side_effects=True, vmem_limit_bytes=32 * 1024 * 1024
        ),
    )(green_blocks, coupling, source, interior_count)
    orbital = lax.axis_index("row") * rows + lax.iota(jnp.int32, rows)
    live = ((orbital < w + interior_count[0]) | (orbital >= width - w)).astype(F32)
    return result * live[None, :, None]


def solution(mesh):
    placed = (
        P(None, ("energy", "slab", "row"), None),
        P(None, "slab", None),
        P(None, ("energy", "slab", "row"), None),
        P("slab"),
    )
    return jax.shard_map(
        body,
        mesh=mesh,
        in_specs=placed,
        out_specs=P(None, ("energy", "slab", "row"), None),
        check_vma=False,
    )
```

```python
import functools

import jax
import jax.numpy as jnp
from jax import lax
from jax.experimental import pallas as pl
from jax.experimental.pallas import tpu as pltpu
from jax.sharding import PartitionSpec as P

F32 = jnp.float32
BF16 = jnp.bfloat16

SOURCE, COUPLE, EDGE, MAP_A, TERM_A, BACK_B, CROSS_B, FIRST_B, STATE, LOWER, AFTER, UPPER = range(12)
(S_SOURCE, S_COUPLE, S_EDGE, S_0, S_1, S_2, S_3, S_LOWER, S_UPPER) = range(9)


def dot(a, b):
    return jnp.dot(a, b, preferred_element_type=F32)


def embed(real, imag):
    return jnp.concatenate(
        [jnp.concatenate([real, -imag], axis=1), jnp.concatenate([imag, real], axis=1)], axis=0
    )


def halves(x):
    high = x.astype(BF16)
    return high, (x - high.astype(F32)).astype(BF16)


def wide_map(x):
    w = x.shape[0] // 2
    high, low = halves(x)
    return embed(high[:w], high[w:]), embed(low[:w], low[w:])


def apply_exact(matrix, x):
    c = x.shape[1]
    y = dot(matrix, jnp.concatenate(halves(x), axis=1))
    return y[:, :c] + y[:, c:]


def apply_wide(matrix, x):
    c = x.shape[1]
    high, low = halves(x)
    y = dot(matrix[0], jnp.concatenate([high, low], axis=1))
    return y[:, :c] + (y[:, c:] + dot(matrix[1], high))


def apply_rounded(matrix, x):
    return dot(matrix[0], x) + dot(matrix[1], x)


def kernel(
    count, green_hbm, couple_hbm, source_hbm, interior_ref, out_ref,
    green, couple, source, source_in, couple_in, edge_in, map_a, term_a, back_b, cross_b, first_b,
    state, lower, after, upper, edge_out, out_0, out_1, out_2, ship, low_out, up_out,
    copy_sem, send_sem, recv_sem,
):
    rows, width = green.shape[1], green.shape[2]
    w = couple.shape[1]
    cols = source.shape[2]
    s = lax.axis_index("slab")
    r = lax.axis_index("row")
    odd = lax.rem(s, 2)
    pair = s // 2
    pairs = count // 2

    loads = [
        pltpu.make_async_copy(source_hbm, source, copy_sem.at[0]),
        pltpu.make_async_copy(green_hbm, green, copy_sem.at[1]),
        pltpu.make_async_copy(couple_hbm, couple, copy_sem.at[2]),
    ]
    for load in loads:
        load.start()

    buffers = [source_in, couple_in, edge_in, map_a, term_a, back_b, cross_b, first_b, state, lower, after, upper]

    def push(src, slot, out_slot, slab, row):
        copy = pltpu.make_async_remote_copy(
            src_ref=src, dst_ref=buffers[slot], send_sem=send_sem.at[out_slot], recv_sem=recv_sem.at[slot],
            device_id={"slab": slab, "row": row}, device_id_type=pl.DeviceIdType.MESH,
        )
        copy.start()
        return copy

    def arrived(slot):
        pltpu.make_async_remote_copy(
            src_ref=buffers[slot], dst_ref=buffers[slot], send_sem=send_sem.at[0], recv_sem=recv_sem.at[slot],
            device_id={"slab": s, "row": 1 - r}, device_id_type=pl.DeviceIdType.MESH,
        ).wait_recv()

    def sent(src, out_slot):
        pltpu.make_async_remote_copy(
            src_ref=src, dst_ref=src, send_sem=send_sem.at[out_slot], recv_sem=recv_sem.at[0],
            device_id={"slab": s, "row": 1 - r}, device_id_type=pl.DeviceIdType.MESH,
        ).wait_send()

    barrier = pltpu.get_barrier_semaphore()
    leader = jnp.logical_or(jnp.logical_and(odd == 0, r == 0), jnp.logical_and(odd == 1, r == 1))
    side = jnp.where(r == 1, s + 1, s - 1)
    partners = [
        (s, 1 - r, None),
        (s - 1, r, s > 0),
        (s + 1, r, s < count - 1),
        (side, 1 - r, jnp.logical_and(side >= 0, side < count)),
        (s - 2, r, jnp.logical_and(leader, s >= 2)),
        (s + 2, r, jnp.logical_and(leader, s < count - 2)),
        (jnp.where(odd == 1, s - 1, s + 1), 1 - r, leader),
    ]
    expected = 1
    for slab, row, there in partners:
        def greet(slab=slab, row=row):
            pl.semaphore_signal(
                barrier, inc=1, device_id={"slab": slab, "row": row}, device_id_type=pl.DeviceIdType.MESH
            )
        if there is None:
            greet()
        else:
            pl.when(there)(greet)
            expected = expected + there.astype(jnp.int32)
    pl.semaphore_wait(barrier, expected)

    push(source_hbm, SOURCE, S_SOURCE, s, 1 - r)

    @pl.when(s < count - 1)
    def _():
        push(couple_hbm, COUPLE, S_COUPLE, s + 1, r)

    interior = interior_ref[0]

    def injected(ref, half):
        orbital = half * rows + lax.broadcasted_iota(jnp.int32, (rows, cols), 0)
        live = jnp.logical_or(orbital < w + interior, orbital >= width - w).astype(F32)
        return jnp.concatenate(
            [(ref[0].astype(F32) * live).astype(BF16), (ref[1].astype(F32) * live).astype(BF16)], axis=1
        )

    def add_product(x, columns, first):
        by_real = dot(green[0, :, columns], x)
        by_imag = dot(green[1, :, columns], x)
        real = by_real[:, :cols] - by_imag[:, cols:]
        imag = by_real[:, cols:] + by_imag[:, :cols]
        if first:
            out_ref[0], out_ref[1] = real, imag
        else:
            out_ref[0] += real
            out_ref[1] += imag

    loads[0].wait()
    loads[1].wait()
    add_product(injected(source, r), pl.ds(pl.multiple_of(r * rows, w), rows), True)
    arrived(SOURCE)
    add_product(injected(source_in, 1 - r), pl.ds(pl.multiple_of((1 - r) * rows, w), rows), False)

    loads[2].wait()
    head, tail = slice(0, w), slice(width - w, width)
    has_next = (s < count - 1).astype(F32)

    def next_coupling():
        return (couple[...].astype(F32) * has_next).astype(BF16).reshape(2 * w, w)

    def previous_coupling():
        @pl.when(s > 0)
        def _():
            arrived(COUPLE)

        @pl.when(s == 0)
        def _():
            couple_in[...] = jnp.zeros_like(couple_in)

    def previous_adjoint():
        return (
            couple_in[0].astype(F32).T.astype(BF16),
            (-couple_in[1].astype(F32).T).astype(BF16),
        )

    def block(first_row, columns):
        return embed(
            green[0, first_row:first_row + w, columns], green[1, first_row:first_row + w, columns]
        )

    def surface(first_row):
        return jnp.concatenate(
            [out_ref[0, first_row:first_row + w, :], out_ref[1, first_row:first_row + w, :]], axis=0
        )

    def pairwise(ref):
        return jnp.concatenate([ref[:w], ref[w:]], axis=1)

    def no_state(ref, there, slot):
        @pl.when(there)
        def _():
            arrived(slot)

        @pl.when(jnp.logical_not(there))
        def _():
            ref[...] = jnp.zeros_like(ref)

    def row_zero(even):
        first = surface(0)
        edge_out[...] = first.astype(BF16)

        @pl.when(s > 0)
        def _():
            push(edge_out, EDGE, S_EDGE, s - 1, 1)

        if not even:
            out_0[...] = first
            push(out_0, FIRST_B, S_0, s - 1, 0)
        couple_now = next_coupling()
        back = dot(block(0, tail), couple_now)
        if not even:
            out_1[...] = back
            push(out_1, BACK_B, S_1, s - 1, 0)
        previous_coupling()
        adj_real, adj_imag = previous_adjoint()
        adjoint = embed(adj_real, adj_imag)
        cross = dot(block(0, head), jnp.concatenate([adj_real, adj_imag], axis=0))
        if not even:
            out_2[...] = cross
            push(out_2, CROSS_B, S_2, s - 1, 0)
            couple_map = embed(couple_now[:w], couple_now[w:])
        else:
            couple_map = embed(couple_now[:w], couple_now[w:])
            arrived(BACK_B)
            back_own = wide_map(back)
            back_two = wide_map(apply_wide(back_own, back_b[...]))
            back_far = wide_map(back_b[...])
            arrived(CROSS_B)
            arrived(MAP_A)
            cross_far = wide_map(cross_b[...])
            cross_two_f = apply_wide(cross_far, map_a[...])
            cross_two = wide_map(cross_two_f)
            cross_all = wide_map(cross + apply_wide(back_own, cross_two_f))
            arrived(FIRST_B)
            arrived(TERM_A)
            term_b = first_b[...] + apply_rounded(cross_far, term_a[...])
            term = first + apply_wide(back_own, term_b)
            no_state(state, pair > 0, STATE)
            before = state[...]
            term = term + apply_rounded(cross_all, before)

            @pl.when(pair == pairs - 1)
            def _():
                ship[...] = term.astype(BF16)
                push(ship, AFTER, S_0, s - 2, 0)
                push(state, STATE, S_2, s + 1, 1)

            low_out[...] = dot(adjoint, before).astype(BF16)
            push(low_out, LOWER, S_LOWER, s, 1)
            after_own = term_b + apply_rounded(cross_two, before)
            add_product(pairwise(low_out), head, False)
            no_state(after, pair < pairs - 1, AFTER)
            follow = after[...]

            @pl.when(jnp.logical_and(pair > 0, pair < pairs - 1))
            def _():
                ship[...] = (term + apply_rounded(back_two, follow)).astype(BF16)
                push(ship, AFTER, S_0, s - 2, 0)
                push(after, AFTER, S_2, s + 1, 0)

            @pl.when(pair == 1)
            def _():
                push(ship, AFTER, S_1, s - 1, 0)

            up_out[...] = apply_exact(couple_map, after_own + apply_rounded(back_far, follow)).astype(BF16)
            push(up_out, UPPER, S_UPPER, s, 1)
            add_product(pairwise(up_out), tail, False)
            sent(low_out, S_LOWER)
        if not even:
            arrived(LOWER)
            add_product(pairwise(lower), head, False)
            no_state(after, pair < pairs - 1, AFTER)
            up_out[...] = dot(couple_map, after[...]).astype(BF16)
            push(up_out, UPPER, S_UPPER, s, 1)
            add_product(pairwise(up_out), tail, False)
        sent(up_out, S_UPPER)

        @pl.when(s > 0)
        def _():
            sent(edge_out, S_EDGE)

        if even:
            @pl.when(pair > 0)
            def _():
                sent(ship, S_0)
                sent(ship, S_2)

            @pl.when(pair == 1)
            def _():
                sent(ship, S_1)
        else:
            sent(out_0, S_0)
            sent(out_1, S_1)
            sent(out_2, S_2)

    def row_one(even):
        last = surface(rows - w)
        previous_coupling()
        adj_real, adj_imag = previous_adjoint()
        forward = dot(block(rows - w, head), jnp.concatenate([adj_real, adj_imag], axis=0))
        if even:
            out_0[...] = forward
            push(out_0, MAP_A, S_0, s, 0)
            push(out_0, MAP_A, S_1, s + 1, 1)
        else:
            own = wide_map(forward)
        turned = wide_map(dot(block(rows - w, tail), next_coupling()))
        if even:
            arrived(EDGE)
            edge = edge_in[...]
        else:
            no_state(edge_in, s < count - 1, EDGE)
            edge = edge_in[...]
        term = last + dot(turned[0], edge) + dot(turned[1], edge)
        if even:
            ship[...] = term.astype(BF16)
            push(ship, TERM_A, S_2, s + 1, 1)
            push(ship, TERM_A, S_3, s, 0)
        else:
            arrived(MAP_A)
            both = wide_map(apply_wide(own, map_a[...]))
            near = wide_map(map_a[...])
            arrived(TERM_A)
            total = term + apply_rounded(own, term_a[...])
            no_state(state, pair > 0, STATE)
            before = state[...]

            @pl.when(pair < pairs - 1)
            def _():
                ship[...] = (total + apply_rounded(both, before)).astype(BF16)

            @pl.when(pair == pairs - 2)
            def _():
                push(ship, STATE, S_0, s + 1, 0)

            @pl.when(pair < pairs - 2)
            def _():
                push(ship, STATE, S_0, s + 2, 1)

            @pl.when(jnp.logical_and(pair > 0, pair < pairs - 1))
            def _():
                push(state, STATE, S_1, s - 1, 0)

            inner = term_a[...].astype(F32) + apply_rounded(near, before)
            low_out[...] = apply_exact(embed(adj_real, adj_imag), inner).astype(BF16)
            push(low_out, LOWER, S_LOWER, s, 0)
            add_product(pairwise(low_out), head, False)
        if even:
            arrived(LOWER)
            add_product(pairwise(lower), head, False)
        arrived(UPPER)
        add_product(pairwise(upper), tail, False)
        if even:
            sent(out_0, S_0)
            sent(out_0, S_1)
            sent(ship, S_2)
            sent(ship, S_3)
        else:
            @pl.when(pair < pairs - 1)
            def _():
                sent(ship, S_0)

            @pl.when(jnp.logical_and(pair > 0, pair < pairs - 1))
            def _():
                sent(state, S_1)

            sent(low_out, S_LOWER)

    for row, role in ((0, row_zero), (1, row_one)):
        for parity in (0, 1):
            @pl.when(jnp.logical_and(r == row, odd == parity))
            def _(role=role, parity=parity):
                role(parity == 0)

    sent(source_hbm, S_SOURCE)

    @pl.when(s < count - 1)
    def _():
        sent(couple_hbm, S_COUPLE)


def body(green_blocks, coupling, source, interior_count):
    rows, width = green_blocks.shape[1:]
    w = coupling.shape[1]
    cols = source.shape[2]
    block = pltpu.VMEM((2 * w, cols), F32)
    small = pltpu.VMEM((2 * w, cols), BF16)
    square = pltpu.VMEM((2 * w, w), F32)
    result = pl.pallas_call(
        functools.partial(kernel, lax.axis_size("slab")),
        out_shape=jax.ShapeDtypeStruct((2, rows, cols), F32),
        in_specs=[pl.BlockSpec(memory_space=pltpu.HBM)] * 3 + [pl.BlockSpec(memory_space=pltpu.SMEM)],
        out_specs=pl.BlockSpec(memory_space=pltpu.VMEM),
        scratch_shapes=[
            pltpu.VMEM(green_blocks.shape, BF16),
            pltpu.VMEM(coupling.shape, BF16),
            pltpu.VMEM(source.shape, BF16),
            pltpu.VMEM(source.shape, BF16),
            pltpu.VMEM(coupling.shape, BF16),
            small,
            square,
            small,
            square,
            square,
            block,
            small,
            small,
            small,
            small,
            small,
            block,
            block,
            square,
            small,
            small,
            small,
            pltpu.SemaphoreType.DMA((3,)),
            pltpu.SemaphoreType.DMA((9,)),
            pltpu.SemaphoreType.DMA((12,)),
        ],
        compiler_params=pltpu.CompilerParams(
            collective_id=0, has_side_effects=True, vmem_limit_bytes=60 * 1024 * 1024
        ),
    )(green_blocks, coupling, source, interior_count)
    orbital = lax.axis_index("row") * rows + lax.iota(jnp.int32, rows)
    live = ((orbital < w + interior_count[0]) | (orbital >= width - w)).astype(F32)
    return result * live[None, :, None]


def solution(mesh):
    placed = (
        P(None, ("energy", "slab", "row"), None),
        P(None, "slab", None),
        P(None, ("energy", "slab", "row"), None),
        P("slab"),
    )
    return jax.shard_map(
        body,
        mesh=mesh,
        in_specs=placed,
        out_specs=P(None, ("energy", "slab", "row"), None),
        check_vma=False,
    )
```

```python
import functools

import jax
import jax.numpy as jnp
from jax import lax
from jax.experimental import pallas as pl
from jax.experimental.pallas import tpu as pltpu
from jax.sharding import PartitionSpec as P

F32 = jnp.float32
BF16 = jnp.bfloat16

SOURCE, COUPLE, EDGE, MAP_A, TERM_A, BACK_B, CROSS_B, FIRST_B, STATE, LOWER, AFTER, UPPER = range(12)
(S_SOURCE, S_COUPLE, S_EDGE, S_0, S_1, S_2, S_3, S_LOWER, S_UPPER) = range(9)


def dot(a, b):
    return jnp.dot(a, b, preferred_element_type=F32)


def embed(real, imag):
    return jnp.concatenate(
        [jnp.concatenate([real, -imag], axis=1), jnp.concatenate([imag, real], axis=1)], axis=0
    )


def halves(x):
    high = x.astype(BF16)
    return high, (x - high.astype(F32)).astype(BF16)


def wide_map(x):
    w = x.shape[0] // 2
    high, low = halves(x)
    return embed(high[:w], high[w:]), embed(low[:w], low[w:])


def apply_exact(matrix, x):
    c = x.shape[1]
    y = dot(matrix, jnp.concatenate(halves(x), axis=1))
    return y[:, :c] + y[:, c:]


def apply_wide(matrix, x):
    c = x.shape[1]
    high, low = halves(x)
    y = dot(matrix[0], jnp.concatenate([high, low], axis=1))
    return y[:, :c] + (y[:, c:] + dot(matrix[1], high))


def apply_rounded(matrix, x):
    return dot(matrix[0], x) + dot(matrix[1], x)


def kernel(
    count, green_hbm, couple_hbm, source_hbm, interior_ref, out_ref,
    green, couple, source, source_in, couple_in, edge_in, map_a, term_a, back_b, cross_b, first_b,
    state, lower, after, upper, edge_out, out_0, out_1, out_2, ship, low_out, up_out,
    totals, total_maps, backs, back_maps, ship_map, running,
    copy_sem, send_sem, recv_sem, far_send, far_recv,
):
    rows, width = green.shape[1], green.shape[2]
    w = couple.shape[1]
    cols = source.shape[2]
    s = lax.axis_index("slab")
    r = lax.axis_index("row")
    odd = lax.rem(s, 2)
    pair = s // 2
    pairs = count // 2

    loads = [
        pltpu.make_async_copy(source_hbm, source, copy_sem.at[0]),
        pltpu.make_async_copy(green_hbm, green, copy_sem.at[1]),
        pltpu.make_async_copy(couple_hbm, couple, copy_sem.at[2]),
    ]
    for load in loads:
        load.start()

    buffers = [source_in, couple_in, edge_in, map_a, term_a, back_b, cross_b, first_b, state, lower, after, upper]

    def push(src, slot, out_slot, slab, row):
        copy = pltpu.make_async_remote_copy(
            src_ref=src, dst_ref=buffers[slot], send_sem=send_sem.at[out_slot], recv_sem=recv_sem.at[slot],
            device_id={"slab": slab, "row": row}, device_id_type=pl.DeviceIdType.MESH,
        )
        copy.start()
        return copy

    def far_copy(src, buffer, kind, place, q):
        return pltpu.make_async_remote_copy(
            src_ref=src, dst_ref=buffer.at[place], send_sem=far_send.at[kind % 2, q],
            recv_sem=far_recv.at[kind, place],
            device_id={"slab": 2 * q, "row": 0}, device_id_type=pl.DeviceIdType.MESH,
        )

    def far_push(src, buffer, kind, wanted):
        order = range(pairs) if kind >= 2 else reversed(range(pairs))
        for q in order:
            pl.when(wanted(q))(lambda q=q: far_copy(src, buffer, kind, pair, q).start())

    def far_sent(src, buffer, kind, wanted):
        for q in range(pairs):
            pl.when(wanted(q))(lambda q=q: far_copy(src, buffer, kind, pair, q).wait_send())

    def far_arrived(buffer, kind, place):
        far_copy(buffer.at[place], buffer, kind, place, 0).wait_recv()

    def run(blocks, maps, kind, start, steps, stride):
        running[...] = jnp.zeros_like(running)

        def step(i, carry):
            place = start + stride * i
            far_arrived(blocks, kind, place)

            @pl.when(i > 0)
            def _():
                far_arrived(maps, kind + 1, place)
                matrix = maps[place]
                running[...] = apply_exact(embed(matrix[:w], matrix[w:]), running[...])

            running[...] += blocks[place].astype(F32)
            return carry

        lax.fori_loop(0, steps, step, 0)

    def later_term(q):
        return q > pair

    def later_map(q):
        return jnp.logical_and(pair > 0, q > pair)

    def earlier_term(q):
        return q < pair

    def earlier_map(q):
        return jnp.logical_and(pair < pairs - 1, q < pair)

    def arrived(slot):
        pltpu.make_async_remote_copy(
            src_ref=buffers[slot], dst_ref=buffers[slot], send_sem=send_sem.at[0], recv_sem=recv_sem.at[slot],
            device_id={"slab": s, "row": 1 - r}, device_id_type=pl.DeviceIdType.MESH,
        ).wait_recv()

    def sent(src, out_slot):
        pltpu.make_async_remote_copy(
            src_ref=src, dst_ref=src, send_sem=send_sem.at[out_slot], recv_sem=recv_sem.at[0],
            device_id={"slab": s, "row": 1 - r}, device_id_type=pl.DeviceIdType.MESH,
        ).wait_send()

    barrier = pltpu.get_barrier_semaphore()
    leader = jnp.logical_or(jnp.logical_and(odd == 0, r == 0), jnp.logical_and(odd == 1, r == 1))
    side = jnp.where(r == 1, s + 1, s - 1)
    partners = [
        (s, 1 - r, None),
        (s - 1, r, s > 0),
        (s + 1, r, s < count - 1),
        (side, 1 - r, jnp.logical_and(side >= 0, side < count)),
        (jnp.where(odd == 1, s - 1, s + 1), 1 - r, leader),
    ]
    first_leader = jnp.logical_and(odd == 0, r == 0)
    last_leader = jnp.logical_and(odd == 1, r == 1)
    for q in range(pairs):
        partners.append((2 * q, 0, jnp.logical_and(first_leader, pair != q)))
        partners.append((2 * q + 1, 1, jnp.logical_and(first_leader, q < pair)))
        partners.append((2 * q, 0, jnp.logical_and(last_leader, q > pair)))
    expected = 1
    for slab, row, there in partners:
        def greet(slab=slab, row=row):
            pl.semaphore_signal(
                barrier, inc=1, device_id={"slab": slab, "row": row}, device_id_type=pl.DeviceIdType.MESH
            )
        if there is None:
            greet()
        else:
            pl.when(there)(greet)
            expected = expected + there.astype(jnp.int32)
    pl.semaphore_wait(barrier, expected)

    push(source_hbm, SOURCE, S_SOURCE, s, 1 - r)

    @pl.when(s < count - 1)
    def _():
        push(couple_hbm, COUPLE, S_COUPLE, s + 1, r)

    interior = interior_ref[0]

    def injected(ref, half):
        orbital = half * rows + lax.broadcasted_iota(jnp.int32, (rows, cols), 0)
        live = jnp.logical_or(orbital < w + interior, orbital >= width - w).astype(F32)
        return jnp.concatenate(
            [(ref[0].astype(F32) * live).astype(BF16), (ref[1].astype(F32) * live).astype(BF16)], axis=1
        )

    def add_product(x, columns, first):
        by_real = dot(green[0, :, columns], x)
        by_imag = dot(green[1, :, columns], x)
        real = by_real[:, :cols] - by_imag[:, cols:]
        imag = by_real[:, cols:] + by_imag[:, :cols]
        if first:
            out_ref[0], out_ref[1] = real, imag
        else:
            out_ref[0] += real
            out_ref[1] += imag

    loads[0].wait()
    loads[1].wait()
    add_product(injected(source, r), pl.ds(pl.multiple_of(r * rows, w), rows), True)
    arrived(SOURCE)
    add_product(injected(source_in, 1 - r), pl.ds(pl.multiple_of((1 - r) * rows, w), rows), False)

    loads[2].wait()
    head, tail = slice(0, w), slice(width - w, width)
    has_next = (s < count - 1).astype(F32)

    def next_coupling():
        return (couple[...].astype(F32) * has_next).astype(BF16).reshape(2 * w, w)

    def previous_coupling():
        @pl.when(s > 0)
        def _():
            arrived(COUPLE)

        @pl.when(s == 0)
        def _():
            couple_in[...] = jnp.zeros_like(couple_in)

    def previous_adjoint():
        return (
            couple_in[0].astype(F32).T.astype(BF16),
            (-couple_in[1].astype(F32).T).astype(BF16),
        )

    def block(first_row, columns):
        return embed(
            green[0, first_row:first_row + w, columns], green[1, first_row:first_row + w, columns]
        )

    def surface(first_row):
        return jnp.concatenate(
            [out_ref[0, first_row:first_row + w, :], out_ref[1, first_row:first_row + w, :]], axis=0
        )

    def pairwise(ref):
        return jnp.concatenate([ref[:w], ref[w:]], axis=1)

    def no_state(ref, there, slot):
        @pl.when(there)
        def _():
            arrived(slot)

        @pl.when(jnp.logical_not(there))
        def _():
            ref[...] = jnp.zeros_like(ref)

    def row_zero(even):
        first = surface(0)
        edge_out[...] = first.astype(BF16)

        @pl.when(s > 0)
        def _():
            push(edge_out, EDGE, S_EDGE, s - 1, 1)

        if not even:
            out_0[...] = first
            push(out_0, FIRST_B, S_0, s - 1, 0)
        couple_now = next_coupling()
        back = dot(block(0, tail), couple_now)
        if not even:
            out_1[...] = back
            push(out_1, BACK_B, S_1, s - 1, 0)
        previous_coupling()
        adj_real, adj_imag = previous_adjoint()
        adjoint = embed(adj_real, adj_imag)
        cross = dot(block(0, head), jnp.concatenate([adj_real, adj_imag], axis=0))
        if not even:
            out_2[...] = cross
            push(out_2, CROSS_B, S_2, s - 1, 0)
            couple_map = embed(couple_now[:w], couple_now[w:])
        else:
            couple_map = embed(couple_now[:w], couple_now[w:])
            arrived(BACK_B)
            back_own = wide_map(back)
            ship_map[...] = apply_wide(back_own, back_b[...]).astype(BF16)
            far_push(ship_map, back_maps, 3, earlier_map)
            back_far = wide_map(back_b[...])
            arrived(CROSS_B)
            arrived(MAP_A)
            cross_far = wide_map(cross_b[...])
            cross_two_f = apply_wide(cross_far, map_a[...])
            cross_two = wide_map(cross_two_f)
            cross_all = wide_map(cross + apply_wide(back_own, cross_two_f))
            arrived(FIRST_B)
            arrived(TERM_A)
            term_b = first_b[...] + apply_rounded(cross_far, term_a[...])
            term = first + apply_wide(back_own, term_b)
            run(totals, total_maps, 0, 0, pair, 1)
            before = running[...]
            ship[...] = (term + apply_wide(cross_all, before)).astype(BF16)
            far_push(ship, backs, 2, earlier_term)

            @pl.when(pair > 0)
            def _():
                state[...] = before.astype(BF16)
                push(state, STATE, S_2, s + 1, 1)

            low_out[...] = apply_exact(adjoint, before).astype(BF16)
            push(low_out, LOWER, S_LOWER, s, 1)
            after_own = term_b + apply_wide(cross_two, before)
            add_product(pairwise(low_out), head, False)
            run(backs, back_maps, 2, pairs - 1, pairs - 1 - pair, -1)
            follow = running[...]

            @pl.when(pair < pairs - 1)
            def _():
                after[...] = follow.astype(BF16)
                push(after, AFTER, S_0, s + 1, 0)

            up_out[...] = apply_exact(couple_map, after_own + apply_wide(back_far, follow)).astype(BF16)
            push(up_out, UPPER, S_UPPER, s, 1)
            add_product(pairwise(up_out), tail, False)
            sent(low_out, S_LOWER)
        if not even:
            arrived(LOWER)
            add_product(pairwise(lower), head, False)
            no_state(after, pair < pairs - 1, AFTER)
            up_out[...] = dot(couple_map, after[...]).astype(BF16)
            push(up_out, UPPER, S_UPPER, s, 1)
            add_product(pairwise(up_out), tail, False)
        sent(up_out, S_UPPER)

        @pl.when(s > 0)
        def _():
            sent(edge_out, S_EDGE)

        if even:
            @pl.when(pair > 0)
            def _():
                sent(state, S_2)

            @pl.when(pair < pairs - 1)
            def _():
                sent(after, S_0)

            far_sent(ship_map, back_maps, 3, earlier_map)
            far_sent(ship, backs, 2, earlier_term)
        else:
            sent(out_0, S_0)
            sent(out_1, S_1)
            sent(out_2, S_2)

    def row_one(even):
        last = surface(rows - w)
        previous_coupling()
        adj_real, adj_imag = previous_adjoint()
        forward = dot(block(rows - w, head), jnp.concatenate([adj_real, adj_imag], axis=0))
        if even:
            out_0[...] = forward
            push(out_0, MAP_A, S_0, s, 0)
            push(out_0, MAP_A, S_1, s + 1, 1)
        else:
            own = wide_map(forward)
        turned = wide_map(dot(block(rows - w, tail), next_coupling()))
        if even:
            arrived(EDGE)
            edge = edge_in[...]
        else:
            no_state(edge_in, s < count - 1, EDGE)
            edge = edge_in[...]
        term = last + dot(turned[0], edge) + dot(turned[1], edge)
        if even:
            ship[...] = term.astype(BF16)
            push(ship, TERM_A, S_2, s + 1, 1)
            push(ship, TERM_A, S_3, s, 0)
        else:
            arrived(MAP_A)
            ship_map[...] = apply_wide(own, map_a[...]).astype(BF16)
            far_push(ship_map, total_maps, 1, later_map)
            near = wide_map(map_a[...])
            arrived(TERM_A)
            ship[...] = (term + apply_rounded(own, term_a[...])).astype(BF16)
            far_push(ship, totals, 0, later_term)
            no_state(state, pair > 0, STATE)
            before = state[...]
            inner = term_a[...].astype(F32) + apply_rounded(near, before)
            low_out[...] = apply_exact(embed(adj_real, adj_imag), inner).astype(BF16)
            push(low_out, LOWER, S_LOWER, s, 0)
            add_product(pairwise(low_out), head, False)
        if even:
            arrived(LOWER)
            add_product(pairwise(lower), head, False)
        arrived(UPPER)
        add_product(pairwise(upper), tail, False)
        if even:
            sent(out_0, S_0)
            sent(out_0, S_1)
            sent(ship, S_2)
            sent(ship, S_3)
        else:
            far_sent(ship_map, total_maps, 1, later_map)
            far_sent(ship, totals, 0, later_term)
            sent(low_out, S_LOWER)

    for row, role in ((0, row_zero), (1, row_one)):
        for parity in (0, 1):
            @pl.when(jnp.logical_and(r == row, odd == parity))
            def _(role=role, parity=parity):
                role(parity == 0)

    sent(source_hbm, S_SOURCE)

    @pl.when(s < count - 1)
    def _():
        sent(couple_hbm, S_COUPLE)


def body(green_blocks, coupling, source, interior_count):
    rows, width = green_blocks.shape[1:]
    w = coupling.shape[1]
    cols = source.shape[2]
    block = pltpu.VMEM((2 * w, cols), F32)
    small = pltpu.VMEM((2 * w, cols), BF16)
    square = pltpu.VMEM((2 * w, w), F32)
    pairs = lax.axis_size("slab") // 2
    result = pl.pallas_call(
        functools.partial(kernel, lax.axis_size("slab")),
        out_shape=jax.ShapeDtypeStruct((2, rows, cols), F32),
        in_specs=[pl.BlockSpec(memory_space=pltpu.HBM)] * 3 + [pl.BlockSpec(memory_space=pltpu.SMEM)],
        out_specs=pl.BlockSpec(memory_space=pltpu.VMEM),
        scratch_shapes=[
            pltpu.VMEM(green_blocks.shape, BF16),
            pltpu.VMEM(coupling.shape, BF16),
            pltpu.VMEM(source.shape, BF16),
            pltpu.VMEM(source.shape, BF16),
            pltpu.VMEM(coupling.shape, BF16),
            small,
            square,
            small,
            square,
            square,
            block,
            small,
            small,
            small,
            small,
            small,
            block,
            block,
            square,
            small,
            small,
            small,
            pltpu.VMEM((pairs, 2 * w, cols), BF16),
            pltpu.VMEM((pairs, 2 * w, w), BF16),
            pltpu.VMEM((pairs, 2 * w, cols), BF16),
            pltpu.VMEM((pairs, 2 * w, w), BF16),
            pltpu.VMEM((2 * w, w), BF16),
            block,
            pltpu.SemaphoreType.DMA((3,)),
            pltpu.SemaphoreType.DMA((9,)),
            pltpu.SemaphoreType.DMA((12,)),
            pltpu.SemaphoreType.DMA((2, pairs)),
            pltpu.SemaphoreType.DMA((4, pairs)),
        ],
        compiler_params=pltpu.CompilerParams(
            collective_id=0, has_side_effects=True, vmem_limit_bytes=60 * 1024 * 1024
        ),
    )(green_blocks, coupling, source, interior_count)
    orbital = lax.axis_index("row") * rows + lax.iota(jnp.int32, rows)
    live = ((orbital < w + interior_count[0]) | (orbital >= width - w)).astype(F32)
    return result * live[None, :, None]


def solution(mesh):
    placed = (
        P(None, ("energy", "slab", "row"), None),
        P(None, "slab", None),
        P(None, ("energy", "slab", "row"), None),
        P("slab"),
    )
    return jax.shard_map(
        body,
        mesh=mesh,
        in_specs=placed,
        out_specs=P(None, ("energy", "slab", "row"), None),
        check_vma=False,
    )
```

```python
import functools

import jax
import jax.numpy as jnp
from jax import lax
from jax.experimental import pallas as pl
from jax.experimental.pallas import tpu as pltpu
from jax.sharding import PartitionSpec as P

F32 = jnp.float32
BF16 = jnp.bfloat16

SOURCE, COUPLE, EDGE, MAP_A, TERM_A, BACK_B, CROSS_B, FIRST_B, STATE, LOWER, AFTER, UPPER = range(12)
(S_SOURCE, S_COUPLE, S_EDGE, S_0, S_1, S_2, S_3, S_LOWER, S_UPPER) = range(9)


def dot(a, b):
    return jnp.dot(a, b, preferred_element_type=F32)


def embed(real, imag):
    return jnp.concatenate(
        [jnp.concatenate([real, -imag], axis=1), jnp.concatenate([imag, real], axis=1)], axis=0
    )


def halves(x):
    high = x.astype(BF16)
    return high, (x - high.astype(F32)).astype(BF16)


def wide_map(x):
    w = x.shape[0] // 2
    high, low = halves(x)
    return embed(high[:w], high[w:]), embed(low[:w], low[w:])


def apply_exact(matrix, x):
    c = x.shape[1]
    y = dot(matrix, jnp.concatenate(halves(x), axis=1))
    return y[:, :c] + y[:, c:]


def apply_wide(matrix, x):
    c = x.shape[1]
    high, low = halves(x)
    y = dot(matrix[0], jnp.concatenate([high, low], axis=1))
    return y[:, :c] + (y[:, c:] + dot(matrix[1], high))


def apply_rounded(matrix, x):
    return dot(matrix[0], x) + dot(matrix[1], x)


def kernel(
    count, green_hbm, couple_hbm, source_hbm, interior_ref, out_ref,
    green, couple, source, source_in, couple_in, edge_in, map_a, term_a, back_b, cross_b, first_b,
    state, lower, after, upper, edge_out, out_0, out_1, out_2, ship, low_out, up_out,
    totals, total_maps, backs, back_maps, ship_map, running,
    copy_sem, send_sem, recv_sem, far_send, far_recv,
):
    rows, width = green.shape[1], green.shape[2]
    w = couple.shape[1]
    cols = source.shape[2]
    s = lax.axis_index("slab")
    r = lax.axis_index("row")
    odd = lax.rem(s, 2)
    pair = s // 2
    pairs = count // 2

    loads = [
        pltpu.make_async_copy(source_hbm, source, copy_sem.at[0]),
        pltpu.make_async_copy(green_hbm, green, copy_sem.at[1]),
        pltpu.make_async_copy(couple_hbm, couple, copy_sem.at[2]),
    ]
    for load in loads:
        load.start()

    buffers = [source_in, couple_in, edge_in, map_a, term_a, back_b, cross_b, first_b, state, lower, after, upper]

    def push(src, slot, out_slot, slab, row):
        copy = pltpu.make_async_remote_copy(
            src_ref=src, dst_ref=buffers[slot], send_sem=send_sem.at[out_slot], recv_sem=recv_sem.at[slot],
            device_id={"slab": slab, "row": row}, device_id_type=pl.DeviceIdType.MESH,
        )
        copy.start()
        return copy

    def far_copy(src, buffer, kind, place, q):
        return pltpu.make_async_remote_copy(
            src_ref=src, dst_ref=buffer.at[place], send_sem=far_send.at[kind % 2, q],
            recv_sem=far_recv.at[kind, place],
            device_id={"slab": 2 * q, "row": 0}, device_id_type=pl.DeviceIdType.MESH,
        )

    def far_push(src, buffer, kind, wanted):
        order = range(pairs) if kind >= 2 else reversed(range(pairs))
        for q in order:
            pl.when(wanted(q))(lambda q=q: far_copy(src, buffer, kind, pair, q).start())

    def far_sent(src, buffer, kind, wanted):
        for q in range(pairs):
            pl.when(wanted(q))(lambda q=q: far_copy(src, buffer, kind, pair, q).wait_send())

    def far_arrived(buffer, kind, place):
        far_copy(buffer.at[place], buffer, kind, place, 0).wait_recv()

    def run(blocks, maps, kind, start, steps, stride):
        running[...] = jnp.zeros_like(running)

        def step(i, carry):
            place = start + stride * i
            far_arrived(blocks, kind, place)

            @pl.when(i > 0)
            def _():
                far_arrived(maps, kind + 1, place)
                matrix = maps[place]
                running[...] = apply_exact(embed(matrix[:w], matrix[w:]), running[...])

            running[...] += blocks[place].astype(F32)
            return carry

        lax.fori_loop(0, steps, step, 0)

    def later_term(q):
        return q > pair

    def later_map(q):
        return jnp.logical_and(pair > 0, q > pair)

    def earlier_term(q):
        return q < pair

    def earlier_map(q):
        return jnp.logical_and(pair < pairs - 1, q < pair)

    def arrived(slot):
        pltpu.make_async_remote_copy(
            src_ref=buffers[slot], dst_ref=buffers[slot], send_sem=send_sem.at[0], recv_sem=recv_sem.at[slot],
            device_id={"slab": s, "row": 1 - r}, device_id_type=pl.DeviceIdType.MESH,
        ).wait_recv()

    def sent(src, out_slot):
        pltpu.make_async_remote_copy(
            src_ref=src, dst_ref=src, send_sem=send_sem.at[out_slot], recv_sem=recv_sem.at[0],
            device_id={"slab": s, "row": 1 - r}, device_id_type=pl.DeviceIdType.MESH,
        ).wait_send()

    barrier = pltpu.get_barrier_semaphore()
    leader = jnp.logical_or(jnp.logical_and(odd == 0, r == 0), jnp.logical_and(odd == 1, r == 1))
    side = jnp.where(r == 1, s + 1, s - 1)
    partners = [
        (s, 1 - r, None),
        (s - 1, r, s > 0),
        (s + 1, r, s < count - 1),
        (side, 1 - r, jnp.logical_and(side >= 0, side < count)),
        (jnp.where(odd == 1, s - 1, s + 1), 1 - r, leader),
    ]
    first_leader = jnp.logical_and(odd == 0, r == 0)
    last_leader = jnp.logical_and(odd == 1, r == 1)
    for q in range(pairs):
        partners.append((2 * q, 0, jnp.logical_and(first_leader, pair != q)))
        partners.append((2 * q + 1, 1, jnp.logical_and(first_leader, q < pair)))
        partners.append((2 * q, 0, jnp.logical_and(last_leader, q > pair)))
    expected = 1
    for slab, row, there in partners:
        def greet(slab=slab, row=row):
            pl.semaphore_signal(
                barrier, inc=1, device_id={"slab": slab, "row": row}, device_id_type=pl.DeviceIdType.MESH
            )
        if there is None:
            greet()
        else:
            pl.when(there)(greet)
            expected = expected + there.astype(jnp.int32)
    pl.semaphore_wait(barrier, expected)

    push(source_hbm, SOURCE, S_SOURCE, s, 1 - r)

    @pl.when(s < count - 1)
    def _():
        push(couple_hbm, COUPLE, S_COUPLE, s + 1, r)

    interior = interior_ref[0]

    def injected(ref, half):
        orbital = half * rows + lax.broadcasted_iota(jnp.int32, (rows, cols), 0)
        live = jnp.logical_or(orbital < w + interior, orbital >= width - w).astype(F32)
        return jnp.concatenate(
            [(ref[0].astype(F32) * live).astype(BF16), (ref[1].astype(F32) * live).astype(BF16)], axis=1
        )

    def add_product(x, columns, first):
        by_real = dot(green[0, :, columns], x)
        by_imag = dot(green[1, :, columns], x)
        real = by_real[:, :cols] - by_imag[:, cols:]
        imag = by_real[:, cols:] + by_imag[:, :cols]
        if first:
            out_ref[0], out_ref[1] = real, imag
        else:
            out_ref[0] += real
            out_ref[1] += imag

    loads[0].wait()
    loads[1].wait()
    add_product(injected(source, r), pl.ds(pl.multiple_of(r * rows, w), rows), True)
    arrived(SOURCE)
    add_product(injected(source_in, 1 - r), pl.ds(pl.multiple_of((1 - r) * rows, w), rows), False)

    loads[2].wait()
    head, tail = slice(0, w), slice(width - w, width)
    has_next = (s < count - 1).astype(F32)

    def next_coupling():
        return (couple[...].astype(F32) * has_next).astype(BF16).reshape(2 * w, w)

    def previous_coupling():
        @pl.when(s > 0)
        def _():
            arrived(COUPLE)

        @pl.when(s == 0)
        def _():
            couple_in[...] = jnp.zeros_like(couple_in)

    def previous_adjoint():
        return (
            couple_in[0].astype(F32).T.astype(BF16),
            (-couple_in[1].astype(F32).T).astype(BF16),
        )

    def block(first_row, columns):
        return embed(
            green[0, first_row:first_row + w, columns], green[1, first_row:first_row + w, columns]
        )

    def surface(first_row):
        return jnp.concatenate(
            [out_ref[0, first_row:first_row + w, :], out_ref[1, first_row:first_row + w, :]], axis=0
        )

    def pairwise(ref):
        return jnp.concatenate([ref[:w], ref[w:]], axis=1)

    def no_state(ref, there, slot):
        @pl.when(there)
        def _():
            arrived(slot)

        @pl.when(jnp.logical_not(there))
        def _():
            ref[...] = jnp.zeros_like(ref)

    def row_zero(even):
        first = surface(0)
        edge_out[...] = first.astype(BF16)

        @pl.when(s > 0)
        def _():
            push(edge_out, EDGE, S_EDGE, s - 1, 1)

        if not even:
            out_0[...] = first
            push(out_0, FIRST_B, S_0, s - 1, 0)
        couple_now = next_coupling()
        back = dot(block(0, tail), couple_now)
        if not even:
            out_1[...] = back
            push(out_1, BACK_B, S_1, s - 1, 0)
        previous_coupling()
        adj_real, adj_imag = previous_adjoint()
        adjoint = embed(adj_real, adj_imag)
        cross = dot(block(0, head), jnp.concatenate([adj_real, adj_imag], axis=0))
        if not even:
            out_2[...] = cross
            push(out_2, CROSS_B, S_2, s - 1, 0)
            couple_map = embed(couple_now[:w], couple_now[w:])
        else:
            couple_map = embed(couple_now[:w], couple_now[w:])
            arrived(BACK_B)
            back_own = wide_map(back)
            ship_map[...] = apply_wide(back_own, back_b[...]).astype(BF16)
            far_push(ship_map, back_maps, 3, earlier_map)
            back_far = wide_map(back_b[...])
            arrived(CROSS_B)
            arrived(MAP_A)
            cross_far = wide_map(cross_b[...])
            cross_two_f = apply_wide(cross_far, map_a[...])
            cross_two = wide_map(cross_two_f)
            cross_all = wide_map(cross + apply_wide(back_own, cross_two_f))
            arrived(FIRST_B)
            arrived(TERM_A)
            term_b = first_b[...] + apply_rounded(cross_far, term_a[...])
            term = first + apply_wide(back_own, term_b)
            run(totals, total_maps, 0, 0, pair, 1)
            before = running[...]
            ship[...] = (term + apply_wide(cross_all, before)).astype(BF16)
            far_push(ship, backs, 2, earlier_term)

            @pl.when(pair > 0)
            def _():
                state[...] = before.astype(BF16)
                push(state, STATE, S_2, s + 1, 1)

            low_out[...] = apply_exact(adjoint, before).astype(BF16)
            push(low_out, LOWER, S_LOWER, s, 1)
            after_own = term_b + apply_wide(cross_two, before)
            add_product(pairwise(low_out), head, False)
            run(backs, back_maps, 2, pairs - 1, pairs - 1 - pair, -1)
            follow = running[...]

            @pl.when(pair < pairs - 1)
            def _():
                after[...] = follow.astype(BF16)
                push(after, AFTER, S_0, s + 1, 0)

            up_out[...] = apply_exact(couple_map, after_own + apply_wide(back_far, follow)).astype(BF16)
            push(up_out, UPPER, S_UPPER, s, 1)
            add_product(pairwise(up_out), tail, False)
            sent(low_out, S_LOWER)
        if not even:
            arrived(LOWER)
            add_product(pairwise(lower), head, False)
            no_state(after, pair < pairs - 1, AFTER)
            up_out[...] = dot(couple_map, after[...]).astype(BF16)
            push(up_out, UPPER, S_UPPER, s, 1)
            add_product(pairwise(up_out), tail, False)
        sent(up_out, S_UPPER)

        @pl.when(s > 0)
        def _():
            sent(edge_out, S_EDGE)

        if even:
            @pl.when(pair > 0)
            def _():
                sent(state, S_2)

            @pl.when(pair < pairs - 1)
            def _():
                sent(after, S_0)

            far_sent(ship_map, back_maps, 3, earlier_map)
            far_sent(ship, backs, 2, earlier_term)
        else:
            sent(out_0, S_0)
            sent(out_1, S_1)
            sent(out_2, S_2)

    def row_one(even):
        last = surface(rows - w)
        previous_coupling()
        adj_real, adj_imag = previous_adjoint()
        forward = dot(block(rows - w, head), jnp.concatenate([adj_real, adj_imag], axis=0))
        if even:
            out_0[...] = forward
            push(out_0, MAP_A, S_0, s, 0)
            push(out_0, MAP_A, S_1, s + 1, 1)
        else:
            own = wide_map(forward)
        turned = wide_map(dot(block(rows - w, tail), next_coupling()))
        if even:
            arrived(EDGE)
            edge = edge_in[...]
        else:
            no_state(edge_in, s < count - 1, EDGE)
            edge = edge_in[...]
        term = last + dot(turned[0], edge) + dot(turned[1], edge)
        if even:
            ship[...] = term.astype(BF16)
            push(ship, TERM_A, S_2, s + 1, 1)
            push(ship, TERM_A, S_3, s, 0)
        else:
            arrived(MAP_A)
            ship_map[...] = apply_wide(own, map_a[...]).astype(BF16)
            far_push(ship_map, total_maps, 1, later_map)
            near = wide_map(map_a[...])
            arrived(TERM_A)
            ship[...] = (term + apply_rounded(own, term_a[...])).astype(BF16)
            far_push(ship, totals, 0, later_term)
            no_state(state, pair > 0, STATE)
            before = state[...]
            inner = term_a[...].astype(F32) + apply_rounded(near, before)
            low_out[...] = apply_exact(embed(adj_real, adj_imag), inner).astype(BF16)
            push(low_out, LOWER, S_LOWER, s, 0)
            add_product(pairwise(low_out), head, False)
        if even:
            arrived(LOWER)
            add_product(pairwise(lower), head, False)
        arrived(UPPER)
        add_product(pairwise(upper), tail, False)
        if even:
            sent(out_0, S_0)
            sent(out_0, S_1)
            sent(ship, S_2)
            sent(ship, S_3)
        else:
            far_sent(ship_map, total_maps, 1, later_map)
            far_sent(ship, totals, 0, later_term)
            sent(low_out, S_LOWER)

    for row, role in ((0, row_zero), (1, row_one)):
        for parity in (0, 1):
            @pl.when(jnp.logical_and(r == row, odd == parity))
            def _(role=role, parity=parity):
                role(parity == 0)

    sent(source_hbm, S_SOURCE)

    @pl.when(s < count - 1)
    def _():
        sent(couple_hbm, S_COUPLE)


def body(green_blocks, coupling, source, interior_count):
    rows, width = green_blocks.shape[1:]
    w = coupling.shape[1]
    cols = source.shape[2]
    block = pltpu.VMEM((2 * w, cols), F32)
    small = pltpu.VMEM((2 * w, cols), BF16)
    square = pltpu.VMEM((2 * w, w), F32)
    pairs = lax.axis_size("slab") // 2
    result = pl.pallas_call(
        functools.partial(kernel, lax.axis_size("slab")),
        out_shape=pltpu.VMEM((2, rows, cols), F32),
        in_specs=[pl.BlockSpec(memory_space=pltpu.HBM)] * 3 + [pl.BlockSpec(memory_space=pltpu.SMEM)],
        out_specs=pl.BlockSpec(memory_space=pltpu.VMEM),
        scratch_shapes=[
            pltpu.VMEM(green_blocks.shape, BF16),
            pltpu.VMEM(coupling.shape, BF16),
            pltpu.VMEM(source.shape, BF16),
            pltpu.VMEM(source.shape, BF16),
            pltpu.VMEM(coupling.shape, BF16),
            small,
            square,
            small,
            square,
            square,
            block,
            small,
            small,
            small,
            small,
            small,
            block,
            block,
            square,
            small,
            small,
            small,
            pltpu.VMEM((pairs, 2 * w, cols), BF16),
            pltpu.VMEM((pairs, 2 * w, w), BF16),
            pltpu.VMEM((pairs, 2 * w, cols), BF16),
            pltpu.VMEM((pairs, 2 * w, w), BF16),
            pltpu.VMEM((2 * w, w), BF16),
            block,
            pltpu.SemaphoreType.DMA((3,)),
            pltpu.SemaphoreType.DMA((9,)),
            pltpu.SemaphoreType.DMA((12,)),
            pltpu.SemaphoreType.DMA((2, pairs)),
            pltpu.SemaphoreType.DMA((4, pairs)),
        ],
        compiler_params=pltpu.CompilerParams(
            collective_id=0, has_side_effects=True, vmem_limit_bytes=60 * 1024 * 1024
        ),
    )(green_blocks, coupling, source, interior_count)
    orbital = lax.axis_index("row") * rows + lax.iota(jnp.int32, rows)
    live = ((orbital < w + interior_count[0]) | (orbital >= width - w)).astype(F32)
    return result * live[None, :, None]


def solution(mesh):
    placed = (
        P(None, ("energy", "slab", "row"), None),
        P(None, "slab", None),
        P(None, ("energy", "slab", "row"), None),
        P("slab"),
    )
    return jax.shard_map(
        body,
        mesh=mesh,
        in_specs=placed,
        out_specs=P(None, ("energy", "slab", "row"), None),
        check_vma=False,
    )
```

```python
import functools

import jax
import jax.numpy as jnp
from jax import lax
from jax.experimental import pallas as pl
from jax.experimental.pallas import tpu as pltpu
from jax.sharding import PartitionSpec as P

F32 = jnp.float32
BF16 = jnp.bfloat16

SOURCE, COUPLE, EDGE, MAP_A, TERM_A, BACK_B, CROSS_B, FIRST_B, STATE, LOWER, AFTER, UPPER = range(12)
(S_SOURCE, S_COUPLE, S_EDGE, S_0, S_1, S_2, S_3, S_LOWER, S_UPPER) = range(9)


def dot(a, b):
    return jnp.dot(a, b, preferred_element_type=F32)


def embed(real, imag):
    return jnp.concatenate(
        [jnp.concatenate([real, -imag], axis=1), jnp.concatenate([imag, real], axis=1)], axis=0
    )


def halves(x):
    high = x.astype(BF16)
    return high, (x - high.astype(F32)).astype(BF16)


def wide_map(x):
    w = x.shape[0] // 2
    high, low = halves(x)
    return embed(high[:w], high[w:]), embed(low[:w], low[w:])


def apply_exact(matrix, x):
    c = x.shape[1]
    y = dot(matrix, jnp.concatenate(halves(x), axis=1))
    return y[:, :c] + y[:, c:]


def apply_wide(matrix, x):
    c = x.shape[1]
    high, low = halves(x)
    y = dot(matrix[0], jnp.concatenate([high, low], axis=1))
    return y[:, :c] + (y[:, c:] + dot(matrix[1], high))


def apply_rounded(matrix, x):
    return dot(matrix[0], x) + dot(matrix[1], x)


def kernel(
    count, green_hbm, couple_hbm, source_hbm, interior_ref, out_ref,
    green, couple, source, source_in, couple_in, edge_in, map_a, term_a, back_b, cross_b, first_b,
    state, lower, after, upper, edge_out, out_0, out_1, out_2, ship, low_out, up_out,
    totals, total_maps, backs, back_maps, ship_map, running,
    copy_sem, send_sem, recv_sem, far_send, far_recv,
):
    rows, width = green.shape[1], green.shape[2]
    w = couple.shape[1]
    cols = source.shape[2]
    s = lax.axis_index("slab")
    r = lax.axis_index("row")
    odd = lax.rem(s, 2)
    pair = s // 2
    pairs = count // 2

    loads = [
        pltpu.make_async_copy(source_hbm, source, copy_sem.at[0]),
        pltpu.make_async_copy(green_hbm, green, copy_sem.at[1]),
        pltpu.make_async_copy(couple_hbm, couple, copy_sem.at[2]),
    ]
    for load in loads:
        load.start()

    buffers = [source_in, couple_in, edge_in, map_a, term_a, back_b, cross_b, first_b, state, lower, after, upper]

    def push(src, slot, out_slot, slab, row):
        copy = pltpu.make_async_remote_copy(
            src_ref=src, dst_ref=buffers[slot], send_sem=send_sem.at[out_slot], recv_sem=recv_sem.at[slot],
            device_id={"slab": slab, "row": row}, device_id_type=pl.DeviceIdType.MESH,
        )
        copy.start()
        return copy

    def far_copy(src, buffer, kind, place, q):
        return pltpu.make_async_remote_copy(
            src_ref=src, dst_ref=buffer.at[place], send_sem=far_send.at[kind % 2, q],
            recv_sem=far_recv.at[kind, place],
            device_id={"slab": 2 * q, "row": 0}, device_id_type=pl.DeviceIdType.MESH,
        )

    def far_push(src, buffer, kind, wanted):
        order = range(pairs) if kind >= 2 else reversed(range(pairs))
        for q in order:
            pl.when(wanted(q))(lambda q=q: far_copy(src, buffer, kind, pair, q).start())

    def far_sent(src, buffer, kind, wanted):
        for q in range(pairs):
            pl.when(wanted(q))(lambda q=q: far_copy(src, buffer, kind, pair, q).wait_send())

    def far_arrived(buffer, kind, place):
        far_copy(buffer.at[place], buffer, kind, place, 0).wait_recv()

    def run(blocks, maps, kind, start, steps, stride):
        running[...] = jnp.zeros_like(running)

        def step(i, carry):
            place = start + stride * i
            far_arrived(blocks, kind, place)

            @pl.when(i > 0)
            def _():
                far_arrived(maps, kind + 1, place)
                matrix = maps[place]
                running[...] = apply_exact(embed(matrix[:w], matrix[w:]), running[...])

            running[...] += blocks[place].astype(F32)
            return carry

        lax.fori_loop(0, steps, step, 0)

    def later_term(q):
        return q > pair

    def later_map(q):
        return jnp.logical_and(pair > 0, q > pair)

    def earlier_term(q):
        return q < pair

    def earlier_map(q):
        return jnp.logical_and(pair < pairs - 1, q < pair)

    def arrived(slot):
        pltpu.make_async_remote_copy(
            src_ref=buffers[slot], dst_ref=buffers[slot], send_sem=send_sem.at[0], recv_sem=recv_sem.at[slot],
            device_id={"slab": s, "row": 1 - r}, device_id_type=pl.DeviceIdType.MESH,
        ).wait_recv()

    def sent(src, out_slot):
        pltpu.make_async_remote_copy(
            src_ref=src, dst_ref=src, send_sem=send_sem.at[out_slot], recv_sem=recv_sem.at[0],
            device_id={"slab": s, "row": 1 - r}, device_id_type=pl.DeviceIdType.MESH,
        ).wait_send()

    barrier = pltpu.get_barrier_semaphore()
    leader = jnp.logical_or(jnp.logical_and(odd == 0, r == 0), jnp.logical_and(odd == 1, r == 1))
    side = jnp.where(r == 1, s + 1, s - 1)
    partners = [
        (s, 1 - r, None),
        (s - 1, r, s > 0),
        (s + 1, r, s < count - 1),
        (side, 1 - r, jnp.logical_and(side >= 0, side < count)),
        (jnp.where(odd == 1, s - 1, s + 1), 1 - r, leader),
    ]
    first_leader = jnp.logical_and(odd == 0, r == 0)
    last_leader = jnp.logical_and(odd == 1, r == 1)
    for q in range(pairs):
        partners.append((2 * q, 0, jnp.logical_and(first_leader, pair != q)))
        partners.append((2 * q + 1, 1, jnp.logical_and(first_leader, q < pair)))
        partners.append((2 * q, 0, jnp.logical_and(last_leader, q > pair)))
    expected = 1
    for slab, row, there in partners:
        def greet(slab=slab, row=row):
            pl.semaphore_signal(
                barrier, inc=1, device_id={"slab": slab, "row": row}, device_id_type=pl.DeviceIdType.MESH
            )
        if there is None:
            greet()
        else:
            pl.when(there)(greet)
            expected = expected + there.astype(jnp.int32)
    pl.semaphore_wait(barrier, expected)

    push(source_hbm, SOURCE, S_SOURCE, s, 1 - r)

    @pl.when(s < count - 1)
    def _():
        push(couple_hbm, COUPLE, S_COUPLE, s + 1, r)

    interior = interior_ref[0]

    def injected(ref, half):
        orbital = half * rows + lax.broadcasted_iota(jnp.int32, (rows, cols), 0)
        live = jnp.logical_or(orbital < w + interior, orbital >= width - w).astype(F32)
        return jnp.concatenate(
            [(ref[0].astype(F32) * live).astype(BF16), (ref[1].astype(F32) * live).astype(BF16)], axis=1
        )

    def add_product(x, columns, first):
        by_real = dot(green[0, :, columns], x)
        by_imag = dot(green[1, :, columns], x)
        real = by_real[:, :cols] - by_imag[:, cols:]
        imag = by_real[:, cols:] + by_imag[:, :cols]
        if first:
            out_ref[0], out_ref[1] = real, imag
        else:
            out_ref[0] += real
            out_ref[1] += imag

    loads[0].wait()
    loads[1].wait()
    add_product(injected(source, r), pl.ds(pl.multiple_of(r * rows, w), rows), True)
    arrived(SOURCE)
    add_product(injected(source_in, 1 - r), pl.ds(pl.multiple_of((1 - r) * rows, w), rows), False)

    loads[2].wait()
    head, tail = slice(0, w), slice(width - w, width)
    has_next = (s < count - 1).astype(F32)

    def next_coupling():
        return (couple[...].astype(F32) * has_next).astype(BF16).reshape(2 * w, w)

    def previous_coupling():
        @pl.when(s > 0)
        def _():
            arrived(COUPLE)

        @pl.when(s == 0)
        def _():
            couple_in[...] = jnp.zeros_like(couple_in)

    def previous_adjoint():
        return (
            couple_in[0].astype(F32).T.astype(BF16),
            (-couple_in[1].astype(F32).T).astype(BF16),
        )

    def block(first_row, columns):
        return embed(
            green[0, first_row:first_row + w, columns], green[1, first_row:first_row + w, columns]
        )

    def surface(first_row):
        return jnp.concatenate(
            [out_ref[0, first_row:first_row + w, :], out_ref[1, first_row:first_row + w, :]], axis=0
        )

    def pairwise(ref):
        return jnp.concatenate([ref[:w], ref[w:]], axis=1)

    def no_state(ref, there, slot):
        @pl.when(there)
        def _():
            arrived(slot)

        @pl.when(jnp.logical_not(there))
        def _():
            ref[...] = jnp.zeros_like(ref)

    def row_zero(even):
        first = surface(0)
        edge_out[...] = first.astype(BF16)

        @pl.when(s > 0)
        def _():
            push(edge_out, EDGE, S_EDGE, s - 1, 1)

        if not even:
            out_0[...] = first
            push(out_0, FIRST_B, S_0, s - 1, 0)
        couple_now = next_coupling()
        back = dot(block(0, tail), couple_now)
        if not even:
            out_1[...] = back.astype(BF16)
            push(out_1, BACK_B, S_1, s - 1, 0)
        previous_coupling()
        adj_real, adj_imag = previous_adjoint()
        adjoint = embed(adj_real, adj_imag)
        cross = dot(block(0, head), jnp.concatenate([adj_real, adj_imag], axis=0))
        if not even:
            out_2[...] = cross.astype(BF16)
            push(out_2, CROSS_B, S_2, s - 1, 0)
            couple_map = embed(couple_now[:w], couple_now[w:])
        else:
            couple_map = embed(couple_now[:w], couple_now[w:])
            arrived(BACK_B)
            back_own = wide_map(back)
            ship_map[...] = apply_rounded(back_own, back_b[...]).astype(BF16)
            far_push(ship_map, back_maps, 3, earlier_map)
            back_far = embed(back_b[:w], back_b[w:])
            arrived(CROSS_B)
            arrived(MAP_A)
            cross_far = embed(cross_b[:w], cross_b[w:])
            cross_two_f = apply_exact(cross_far, map_a[...])
            cross_two = wide_map(cross_two_f)
            cross_all = wide_map(cross + apply_wide(back_own, cross_two_f))
            arrived(FIRST_B)
            arrived(TERM_A)
            term_b = first_b[...] + dot(cross_far, term_a[...])
            term = first + apply_wide(back_own, term_b)
            run(totals, total_maps, 0, 0, pair, 1)
            before = running[...]
            ship[...] = (term + apply_wide(cross_all, before)).astype(BF16)
            far_push(ship, backs, 2, earlier_term)

            @pl.when(pair > 0)
            def _():
                state[...] = before.astype(BF16)
                push(state, STATE, S_2, s + 1, 1)

            low_out[...] = apply_exact(adjoint, before).astype(BF16)
            push(low_out, LOWER, S_LOWER, s, 1)
            after_own = term_b + apply_wide(cross_two, before)
            add_product(pairwise(low_out), head, False)
            run(backs, back_maps, 2, pairs - 1, pairs - 1 - pair, -1)
            follow = running[...]

            @pl.when(pair < pairs - 1)
            def _():
                after[...] = follow.astype(BF16)
                push(after, AFTER, S_0, s + 1, 0)

            up_out[...] = apply_exact(couple_map, after_own + apply_exact(back_far, follow)).astype(BF16)
            push(up_out, UPPER, S_UPPER, s, 1)
            add_product(pairwise(up_out), tail, False)
            sent(low_out, S_LOWER)
        if not even:
            arrived(LOWER)
            add_product(pairwise(lower), head, False)
            no_state(after, pair < pairs - 1, AFTER)
            up_out[...] = dot(couple_map, after[...]).astype(BF16)
            push(up_out, UPPER, S_UPPER, s, 1)
            add_product(pairwise(up_out), tail, False)
        sent(up_out, S_UPPER)

        @pl.when(s > 0)
        def _():
            sent(edge_out, S_EDGE)

        if even:
            @pl.when(pair > 0)
            def _():
                sent(state, S_2)

            @pl.when(pair < pairs - 1)
            def _():
                sent(after, S_0)

            far_sent(ship_map, back_maps, 3, earlier_map)
            far_sent(ship, backs, 2, earlier_term)
        else:
            sent(out_0, S_0)
            sent(out_1, S_1)
            sent(out_2, S_2)

    def row_one(even):
        last = surface(rows - w)
        previous_coupling()
        adj_real, adj_imag = previous_adjoint()
        forward = dot(block(rows - w, head), jnp.concatenate([adj_real, adj_imag], axis=0))
        if even:
            out_0[...] = forward
            push(out_0, MAP_A, S_1, s + 1, 1)
            push(out_0, MAP_A, S_0, s, 0)
        else:
            own = wide_map(forward)
        turned = wide_map(dot(block(rows - w, tail), next_coupling()))
        if even:
            arrived(EDGE)
            edge = edge_in[...]
        else:
            no_state(edge_in, s < count - 1, EDGE)
            edge = edge_in[...]
        term = last + dot(turned[0], edge) + dot(turned[1], edge)
        if even:
            ship[...] = term.astype(BF16)
            push(ship, TERM_A, S_2, s + 1, 1)
            push(ship, TERM_A, S_3, s, 0)
        else:
            arrived(MAP_A)
            ship_map[...] = apply_wide(own, map_a[...]).astype(BF16)
            far_push(ship_map, total_maps, 1, later_map)
            near = wide_map(map_a[...])
            arrived(TERM_A)
            ship[...] = (term + apply_rounded(own, term_a[...])).astype(BF16)
            far_push(ship, totals, 0, later_term)
            no_state(state, pair > 0, STATE)
            before = state[...]
            inner = term_a[...].astype(F32) + apply_rounded(near, before)
            low_out[...] = apply_exact(embed(adj_real, adj_imag), inner).astype(BF16)
            push(low_out, LOWER, S_LOWER, s, 0)
            add_product(pairwise(low_out), head, False)
        if even:
            arrived(LOWER)
            add_product(pairwise(lower), head, False)
        arrived(UPPER)
        add_product(pairwise(upper), tail, False)
        if even:
            sent(out_0, S_0)
            sent(out_0, S_1)
            sent(ship, S_2)
            sent(ship, S_3)
        else:
            far_sent(ship_map, total_maps, 1, later_map)
            far_sent(ship, totals, 0, later_term)
            sent(low_out, S_LOWER)

    for row, role in ((0, row_zero), (1, row_one)):
        for parity in (0, 1):
            @pl.when(jnp.logical_and(r == row, odd == parity))
            def _(role=role, parity=parity):
                role(parity == 0)

    sent(source_hbm, S_SOURCE)

    @pl.when(s < count - 1)
    def _():
        sent(couple_hbm, S_COUPLE)


def body(green_blocks, coupling, source, interior_count):
    rows, width = green_blocks.shape[1:]
    w = coupling.shape[1]
    cols = source.shape[2]
    block = pltpu.VMEM((2 * w, cols), F32)
    small = pltpu.VMEM((2 * w, cols), BF16)
    square = pltpu.VMEM((2 * w, w), F32)
    pairs = lax.axis_size("slab") // 2
    result = pl.pallas_call(
        functools.partial(kernel, lax.axis_size("slab")),
        out_shape=pltpu.VMEM((2, rows, cols), F32),
        in_specs=[pl.BlockSpec(memory_space=pltpu.HBM)] * 3 + [pl.BlockSpec(memory_space=pltpu.SMEM)],
        out_specs=pl.BlockSpec(memory_space=pltpu.VMEM),
        scratch_shapes=[
            pltpu.VMEM(green_blocks.shape, BF16),
            pltpu.VMEM(coupling.shape, BF16),
            pltpu.VMEM(source.shape, BF16),
            pltpu.VMEM(source.shape, BF16),
            pltpu.VMEM(coupling.shape, BF16),
            small,
            square,
            small,
            pltpu.VMEM((2 * w, w), BF16),
            pltpu.VMEM((2 * w, w), BF16),
            block,
            small,
            small,
            small,
            small,
            small,
            block,
            pltpu.VMEM((2 * w, w), BF16),
            pltpu.VMEM((2 * w, w), BF16),
            small,
            small,
            small,
            pltpu.VMEM((pairs, 2 * w, cols), BF16),
            pltpu.VMEM((pairs, 2 * w, w), BF16),
            pltpu.VMEM((pairs, 2 * w, cols), BF16),
            pltpu.VMEM((pairs, 2 * w, w), BF16),
            pltpu.VMEM((2 * w, w), BF16),
            block,
            pltpu.SemaphoreType.DMA((3,)),
            pltpu.SemaphoreType.DMA((9,)),
            pltpu.SemaphoreType.DMA((12,)),
            pltpu.SemaphoreType.DMA((2, pairs)),
            pltpu.SemaphoreType.DMA((4, pairs)),
        ],
        compiler_params=pltpu.CompilerParams(
            collective_id=0, has_side_effects=True, vmem_limit_bytes=60 * 1024 * 1024
        ),
    )(green_blocks, coupling, source, interior_count)
    orbital = lax.axis_index("row") * rows + lax.iota(jnp.int32, rows)
    live = ((orbital < w + interior_count[0]) | (orbital >= width - w)).astype(F32)
    return result * live[None, :, None]


def solution(mesh):
    placed = (
        P(None, ("energy", "slab", "row"), None),
        P(None, "slab", None),
        P(None, ("energy", "slab", "row"), None),
        P("slab"),
    )
    return jax.shard_map(
        body,
        mesh=mesh,
        in_specs=placed,
        out_specs=P(None, ("energy", "slab", "row"), None),
        check_vma=False,
    )
```

```python
import functools

import jax
import jax.numpy as jnp
from jax import lax
from jax.experimental import pallas as pl
from jax.experimental.pallas import tpu as pltpu
from jax.sharding import PartitionSpec as P

F32 = jnp.float32
BF16 = jnp.bfloat16

SOURCE, COUPLE, EDGE, MAP_A, TERM_A, BACK_B, CROSS_B, FIRST_B, STATE, LOWER, AFTER, UPPER = range(12)
(S_SOURCE, S_COUPLE, S_EDGE, S_0, S_1, S_2, S_3, S_LOWER, S_UPPER) = range(9)


def dot(a, b):
    return jnp.dot(a, b, preferred_element_type=F32)


def embed(real, imag):
    return jnp.concatenate(
        [jnp.concatenate([real, -imag], axis=1), jnp.concatenate([imag, real], axis=1)], axis=0
    )


def halves(x):
    high = x.astype(BF16)
    return high, (x - high.astype(F32)).astype(BF16)


def wide_map(x):
    w = x.shape[0] // 2
    high, low = halves(x)
    return embed(high[:w], high[w:]), embed(low[:w], low[w:])


def apply_exact(matrix, x):
    c = x.shape[1]
    y = dot(matrix, jnp.concatenate(halves(x), axis=1))
    return y[:, :c] + y[:, c:]


def apply_wide(matrix, x):
    c = x.shape[1]
    high, low = halves(x)
    y = dot(matrix[0], jnp.concatenate([high, low], axis=1))
    return y[:, :c] + (y[:, c:] + dot(matrix[1], high))


def apply_rounded(matrix, x):
    return dot(matrix[0], x) + dot(matrix[1], x)


def kernel(
    count, green_hbm, couple_hbm, source_hbm, interior_ref, out_ref,
    green, couple, source, source_in, couple_in, edge_in, map_a, term_a, back_b, cross_b, first_b,
    state, lower, after, upper, edge_out, out_0, out_1, out_2, ship, low_out, up_out,
    totals, total_maps, backs, back_maps, ship_map, running,
    copy_sem, send_sem, recv_sem, far_send, far_recv,
):
    rows, width = green.shape[1], green.shape[2]
    w = couple.shape[1]
    cols = source.shape[2]
    s = lax.axis_index("slab")
    r = lax.axis_index("row")
    odd = lax.rem(s, 2)
    pair = s // 2
    pairs = count // 2

    loads = [
        pltpu.make_async_copy(source_hbm, source, copy_sem.at[0]),
        pltpu.make_async_copy(green_hbm, green, copy_sem.at[1]),
        pltpu.make_async_copy(couple_hbm, couple, copy_sem.at[2]),
    ]
    for load in loads:
        load.start()

    buffers = [source_in, couple_in, edge_in, map_a, term_a, back_b, cross_b, first_b, state, lower, after, upper]

    def push(src, slot, out_slot, slab, row):
        copy = pltpu.make_async_remote_copy(
            src_ref=src, dst_ref=buffers[slot], send_sem=send_sem.at[out_slot], recv_sem=recv_sem.at[slot],
            device_id={"slab": slab, "row": row}, device_id_type=pl.DeviceIdType.MESH,
        )
        copy.start()
        return copy

    def far_copy(src, buffer, kind, place, q):
        return pltpu.make_async_remote_copy(
            src_ref=src, dst_ref=buffer.at[place], send_sem=far_send.at[kind % 2, q],
            recv_sem=far_recv.at[kind, place],
            device_id={"slab": 2 * q, "row": 0}, device_id_type=pl.DeviceIdType.MESH,
        )

    def far_push(src, buffer, kind, wanted):
        order = range(pairs) if kind >= 2 else reversed(range(pairs))
        for q in order:
            pl.when(wanted(q))(lambda q=q: far_copy(src, buffer, kind, pair, q).start())

    def far_sent(src, buffer, kind, wanted):
        for q in range(pairs):
            pl.when(wanted(q))(lambda q=q: far_copy(src, buffer, kind, pair, q).wait_send())

    def far_arrived(buffer, kind, place):
        far_copy(buffer.at[place], buffer, kind, place, 0).wait_recv()

    def run(blocks, maps, kind, start, steps, stride):
        running[...] = jnp.zeros_like(running)

        def step(i, carry):
            place = start + stride * i
            far_arrived(blocks, kind, place)

            @pl.when(i > 0)
            def _():
                far_arrived(maps, kind + 1, place)
                matrix = maps[place]
                running[...] = apply_exact(embed(matrix[:w], matrix[w:]), running[...])

            running[...] += blocks[place].astype(F32)
            return carry

        lax.fori_loop(0, steps, step, 0)

    def later_term(q):
        return q > pair

    def later_map(q):
        return jnp.logical_and(pair > 0, q > pair)

    def earlier_term(q):
        return q < pair

    def earlier_map(q):
        return jnp.logical_and(pair < pairs - 1, q < pair)

    def arrived(slot):
        pltpu.make_async_remote_copy(
            src_ref=buffers[slot], dst_ref=buffers[slot], send_sem=send_sem.at[0], recv_sem=recv_sem.at[slot],
            device_id={"slab": s, "row": 1 - r}, device_id_type=pl.DeviceIdType.MESH,
        ).wait_recv()

    def sent(src, out_slot):
        pltpu.make_async_remote_copy(
            src_ref=src, dst_ref=src, send_sem=send_sem.at[out_slot], recv_sem=recv_sem.at[0],
            device_id={"slab": s, "row": 1 - r}, device_id_type=pl.DeviceIdType.MESH,
        ).wait_send()

    barrier = pltpu.get_barrier_semaphore()
    leader = jnp.logical_or(jnp.logical_and(odd == 0, r == 0), jnp.logical_and(odd == 1, r == 1))
    side = jnp.where(r == 1, s + 1, s - 1)
    partners = [
        (s, 1 - r, None),
        (s - 1, r, s > 0),
        (s + 1, r, s < count - 1),
        (side, 1 - r, jnp.logical_and(side >= 0, side < count)),
        (jnp.where(odd == 1, s - 1, s + 1), 1 - r, leader),
    ]
    first_leader = jnp.logical_and(odd == 0, r == 0)
    last_leader = jnp.logical_and(odd == 1, r == 1)
    for q in range(pairs):
        partners.append((2 * q, 0, jnp.logical_and(first_leader, pair != q)))
        partners.append((2 * q + 1, 1, jnp.logical_and(first_leader, q < pair)))
        partners.append((2 * q, 0, jnp.logical_and(last_leader, q > pair)))
    expected = 1
    for slab, row, there in partners:
        def greet(slab=slab, row=row):
            pl.semaphore_signal(
                barrier, inc=1, device_id={"slab": slab, "row": row}, device_id_type=pl.DeviceIdType.MESH
            )
        if there is None:
            greet()
        else:
            pl.when(there)(greet)
            expected = expected + there.astype(jnp.int32)
    pl.semaphore_wait(barrier, expected)

    push(source_hbm, SOURCE, S_SOURCE, s, 1 - r)

    @pl.when(s < count - 1)
    def _():
        push(couple_hbm, COUPLE, S_COUPLE, s + 1, r)

    interior = interior_ref[0]

    def injected(ref, half):
        orbital = half * rows + lax.broadcasted_iota(jnp.int32, (rows, cols), 0)
        live = jnp.logical_or(orbital < w + interior, orbital >= width - w).astype(F32)
        return jnp.concatenate(
            [(ref[0].astype(F32) * live).astype(BF16), (ref[1].astype(F32) * live).astype(BF16)], axis=1
        )

    def add_product(x, columns, first, span=slice(None)):
        by_real = dot(green[0, span, columns], x)
        by_imag = dot(green[1, span, columns], x)
        real = by_real[:, :cols] - by_imag[:, cols:]
        imag = by_real[:, cols:] + by_imag[:, :cols]
        if first:
            out_ref[0], out_ref[1] = real, imag
        else:
            out_ref[0, span, :] += real
            out_ref[1, span, :] += imag

    loads[0].wait()
    loads[1].wait()
    add_product(injected(source, r), pl.ds(pl.multiple_of(r * rows, w), rows), True)
    arrived(SOURCE)

    loads[2].wait()
    head, tail = slice(0, w), slice(width - w, width)
    has_next = (s < count - 1).astype(F32)

    def next_coupling():
        return (couple[...].astype(F32) * has_next).astype(BF16).reshape(2 * w, w)

    def previous_coupling():
        @pl.when(s > 0)
        def _():
            arrived(COUPLE)

        @pl.when(s == 0)
        def _():
            couple_in[...] = jnp.zeros_like(couple_in)

    def previous_adjoint():
        return (
            couple_in[0].astype(F32).T.astype(BF16),
            (-couple_in[1].astype(F32).T).astype(BF16),
        )

    def block(first_row, columns):
        return embed(
            green[0, first_row:first_row + w, columns], green[1, first_row:first_row + w, columns]
        )

    def surface(first_row):
        return jnp.concatenate(
            [out_ref[0, first_row:first_row + w, :], out_ref[1, first_row:first_row + w, :]], axis=0
        )

    def pairwise(ref):
        return jnp.concatenate([ref[:w], ref[w:]], axis=1)

    def no_state(ref, there, slot):
        @pl.when(there)
        def _():
            arrived(slot)

        @pl.when(jnp.logical_not(there))
        def _():
            ref[...] = jnp.zeros_like(ref)

    def row_zero(even):
        there = slice(rows, 2 * rows)
        injection = injected(source_in, 1)
        add_product(injection, there, False, slice(0, w))
        first = surface(0)
        edge_out[...] = first.astype(BF16)

        @pl.when(s > 0)
        def _():
            push(edge_out, EDGE, S_EDGE, s - 1, 1)

        if not even:
            out_0[...] = first
            push(out_0, FIRST_B, S_0, s - 1, 0)
        add_product(injection, there, False, slice(w, rows))
        couple_now = next_coupling()
        back = dot(block(0, tail), couple_now)
        if not even:
            out_1[...] = back
            push(out_1, BACK_B, S_1, s - 1, 0)
        previous_coupling()
        adj_real, adj_imag = previous_adjoint()
        adjoint = embed(adj_real, adj_imag)
        cross = dot(block(0, head), jnp.concatenate([adj_real, adj_imag], axis=0))
        if not even:
            out_2[...] = cross
            push(out_2, CROSS_B, S_2, s - 1, 0)
            couple_map = embed(couple_now[:w], couple_now[w:])
        else:
            couple_map = embed(couple_now[:w], couple_now[w:])
            arrived(BACK_B)
            back_own = wide_map(back)
            ship_map[...] = apply_wide(back_own, back_b[...]).astype(BF16)
            far_push(ship_map, back_maps, 3, earlier_map)
            back_far = wide_map(back_b[...])
            arrived(CROSS_B)
            arrived(MAP_A)
            cross_far = wide_map(cross_b[...])
            cross_two_f = apply_wide(cross_far, map_a[...])
            cross_two = wide_map(cross_two_f)
            cross_all = wide_map(cross + apply_wide(back_own, cross_two_f))
            arrived(FIRST_B)
            arrived(TERM_A)
            term_b = first_b[...] + apply_rounded(cross_far, term_a[...])
            term = first + apply_wide(back_own, term_b)
            run(totals, total_maps, 0, 0, pair, 1)
            before = running[...]
            ship[...] = (term + apply_wide(cross_all, before)).astype(BF16)
            far_push(ship, backs, 2, earlier_term)

            @pl.when(pair > 0)
            def _():
                state[...] = before.astype(BF16)
                push(state, STATE, S_2, s + 1, 1)

            low_out[...] = apply_exact(adjoint, before).astype(BF16)
            push(low_out, LOWER, S_LOWER, s, 1)
            after_own = term_b + apply_wide(cross_two, before)
            add_product(pairwise(low_out), head, False)
            run(backs, back_maps, 2, pairs - 1, pairs - 1 - pair, -1)
            follow = running[...]

            @pl.when(pair < pairs - 1)
            def _():
                after[...] = follow.astype(BF16)
                push(after, AFTER, S_0, s + 1, 0)

            up_out[...] = apply_exact(couple_map, after_own + apply_wide(back_far, follow)).astype(BF16)
            push(up_out, UPPER, S_UPPER, s, 1)
            add_product(pairwise(up_out), tail, False)
            sent(low_out, S_LOWER)
        if not even:
            arrived(LOWER)
            add_product(pairwise(lower), head, False)
            no_state(after, pair < pairs - 1, AFTER)
            up_out[...] = dot(couple_map, after[...]).astype(BF16)
            push(up_out, UPPER, S_UPPER, s, 1)
            add_product(pairwise(up_out), tail, False)
        sent(up_out, S_UPPER)

        @pl.when(s > 0)
        def _():
            sent(edge_out, S_EDGE)

        if even:
            @pl.when(pair > 0)
            def _():
                sent(state, S_2)

            @pl.when(pair < pairs - 1)
            def _():
                sent(after, S_0)

            far_sent(ship_map, back_maps, 3, earlier_map)
            far_sent(ship, backs, 2, earlier_term)
        else:
            sent(out_0, S_0)
            sent(out_1, S_1)
            sent(out_2, S_2)

    def row_one(even):
        add_product(injected(source_in, 0), slice(0, rows), False)
        last = surface(rows - w)
        previous_coupling()
        adj_real, adj_imag = previous_adjoint()
        forward = dot(block(rows - w, head), jnp.concatenate([adj_real, adj_imag], axis=0))
        if even:
            out_0[...] = forward
            push(out_0, MAP_A, S_0, s, 0)
            push(out_0, MAP_A, S_1, s + 1, 1)
        else:
            own = wide_map(forward)
        turned = wide_map(dot(block(rows - w, tail), next_coupling()))
        if even:
            arrived(EDGE)
            edge = edge_in[...]
        else:
            no_state(edge_in, s < count - 1, EDGE)
            edge = edge_in[...]
        term = last + dot(turned[0], edge) + dot(turned[1], edge)
        if even:
            ship[...] = term.astype(BF16)
            push(ship, TERM_A, S_2, s + 1, 1)
            push(ship, TERM_A, S_3, s, 0)
        else:
            arrived(MAP_A)
            ship_map[...] = apply_wide(own, map_a[...]).astype(BF16)
            far_push(ship_map, total_maps, 1, later_map)
            near = wide_map(map_a[...])
            arrived(TERM_A)
            ship[...] = (term + apply_rounded(own, term_a[...])).astype(BF16)
            far_push(ship, totals, 0, later_term)
            no_state(state, pair > 0, STATE)
            before = state[...]
            inner = term_a[...].astype(F32) + apply_rounded(near, before)
            low_out[...] = apply_exact(embed(adj_real, adj_imag), inner).astype(BF16)
            push(low_out, LOWER, S_LOWER, s, 0)
            add_product(pairwise(low_out), head, False)
        if even:
            arrived(LOWER)
            add_product(pairwise(lower), head, False)
        arrived(UPPER)
        add_product(pairwise(upper), tail, False)
        if even:
            sent(out_0, S_0)
            sent(out_0, S_1)
            sent(ship, S_2)
            sent(ship, S_3)
        else:
            far_sent(ship_map, total_maps, 1, later_map)
            far_sent(ship, totals, 0, later_term)
            sent(low_out, S_LOWER)

    for row, role in ((0, row_zero), (1, row_one)):
        for parity in (0, 1):
            @pl.when(jnp.logical_and(r == row, odd == parity))
            def _(role=role, parity=parity):
                role(parity == 0)

    sent(source_hbm, S_SOURCE)

    @pl.when(s < count - 1)
    def _():
        sent(couple_hbm, S_COUPLE)


def body(green_blocks, coupling, source, interior_count):
    rows, width = green_blocks.shape[1:]
    w = coupling.shape[1]
    cols = source.shape[2]
    block = pltpu.VMEM((2 * w, cols), F32)
    small = pltpu.VMEM((2 * w, cols), BF16)
    square = pltpu.VMEM((2 * w, w), F32)
    pairs = lax.axis_size("slab") // 2
    result = pl.pallas_call(
        functools.partial(kernel, lax.axis_size("slab")),
        out_shape=pltpu.VMEM((2, rows, cols), F32),
        in_specs=[pl.BlockSpec(memory_space=pltpu.HBM)] * 3 + [pl.BlockSpec(memory_space=pltpu.SMEM)],
        out_specs=pl.BlockSpec(memory_space=pltpu.VMEM),
        scratch_shapes=[
            pltpu.VMEM(green_blocks.shape, BF16),
            pltpu.VMEM(coupling.shape, BF16),
            pltpu.VMEM(source.shape, BF16),
            pltpu.VMEM(source.shape, BF16),
            pltpu.VMEM(coupling.shape, BF16),
            small,
            square,
            small,
            square,
            square,
            block,
            small,
            small,
            small,
            small,
            small,
            block,
            block,
            square,
            small,
            small,
            small,
            pltpu.VMEM((pairs, 2 * w, cols), BF16),
            pltpu.VMEM((pairs, 2 * w, w), BF16),
            pltpu.VMEM((pairs, 2 * w, cols), BF16),
            pltpu.VMEM((pairs, 2 * w, w), BF16),
            pltpu.VMEM((2 * w, w), BF16),
            block,
            pltpu.SemaphoreType.DMA((3,)),
            pltpu.SemaphoreType.DMA((9,)),
            pltpu.SemaphoreType.DMA((12,)),
            pltpu.SemaphoreType.DMA((2, pairs)),
            pltpu.SemaphoreType.DMA((4, pairs)),
        ],
        compiler_params=pltpu.CompilerParams(
            collective_id=0, has_side_effects=True, vmem_limit_bytes=60 * 1024 * 1024
        ),
    )(green_blocks, coupling, source, interior_count)
    orbital = lax.axis_index("row") * rows + lax.iota(jnp.int32, rows)
    live = ((orbital < w + interior_count[0]) | (orbital >= width - w)).astype(F32)
    return result * live[None, :, None]


def solution(mesh):
    placed = (
        P(None, ("energy", "slab", "row"), None),
        P(None, "slab", None),
        P(None, ("energy", "slab", "row"), None),
        P("slab"),
    )
    return jax.shard_map(
        body,
        mesh=mesh,
        in_specs=placed,
        out_specs=P(None, ("energy", "slab", "row"), None),
        check_vma=False,
    )
```

```python
import functools

import jax
import jax.numpy as jnp
from jax import lax
from jax.experimental import pallas as pl
from jax.experimental.pallas import tpu as pltpu
from jax.sharding import PartitionSpec as P

F32 = jnp.float32
BF16 = jnp.bfloat16

SOURCE, COUPLE, EDGE, MAP_A, TERM_A, BACK_B, CROSS_B, FIRST_B, STATE, LOWER, AFTER, UPPER = range(12)
(S_SOURCE, S_COUPLE, S_EDGE, S_0, S_1, S_2, S_3, S_LOWER, S_UPPER) = range(9)


def dot(a, b):
    return jnp.dot(a, b, preferred_element_type=F32)


def embed(real, imag):
    return jnp.concatenate(
        [jnp.concatenate([real, -imag], axis=1), jnp.concatenate([imag, real], axis=1)], axis=0
    )


def halves(x):
    high = x.astype(BF16)
    return high, (x - high.astype(F32)).astype(BF16)


def wide_map(x):
    w = x.shape[0] // 2
    high, low = halves(x)
    return embed(high[:w], high[w:]), embed(low[:w], low[w:])


def apply_exact(matrix, x):
    c = x.shape[1]
    y = dot(matrix, jnp.concatenate(halves(x), axis=1))
    return y[:, :c] + y[:, c:]


def apply_wide(matrix, x):
    c = x.shape[1]
    high, low = halves(x)
    y = dot(matrix[0], jnp.concatenate([high, low], axis=1))
    return y[:, :c] + (y[:, c:] + dot(matrix[1], high))


def apply_rounded(matrix, x):
    return dot(matrix[0], x) + dot(matrix[1], x)


def kernel(
    count, green_hbm, couple_hbm, source_hbm, interior_ref, out_ref,
    green, couple, source, source_in, couple_in, edge_in, map_a, term_a, back_b, cross_b, first_b,
    state, lower, after, upper, edge_out, out_0, out_1, out_2, ship, low_out, up_out,
    totals, total_maps, backs, back_maps, ship_map, running,
    copy_sem, send_sem, recv_sem, far_send, far_recv,
):
    rows, width = green.shape[1], green.shape[2]
    w = couple.shape[1]
    cols = source.shape[2]
    s = lax.axis_index("slab")
    r = lax.axis_index("row")
    odd = lax.rem(s, 2)
    pair = s // 2
    pairs = count // 2

    loads = [
        pltpu.make_async_copy(source_hbm, source, copy_sem.at[0]),
        pltpu.make_async_copy(green_hbm, green, copy_sem.at[1]),
        pltpu.make_async_copy(couple_hbm, couple, copy_sem.at[2]),
    ]
    for load in loads:
        load.start()

    buffers = [source_in, couple_in, edge_in, map_a, term_a, back_b, cross_b, first_b, state, lower, after, upper]

    def push(src, slot, out_slot, slab, row):
        copy = pltpu.make_async_remote_copy(
            src_ref=src, dst_ref=buffers[slot], send_sem=send_sem.at[out_slot], recv_sem=recv_sem.at[slot],
            device_id={"slab": slab, "row": row}, device_id_type=pl.DeviceIdType.MESH,
        )
        copy.start()
        return copy

    def far_copy(src, buffer, kind, place, q):
        return pltpu.make_async_remote_copy(
            src_ref=src, dst_ref=buffer.at[place], send_sem=far_send.at[kind % 2, q],
            recv_sem=far_recv.at[kind, place],
            device_id={"slab": 2 * q, "row": 0}, device_id_type=pl.DeviceIdType.MESH,
        )

    def far_push(src, buffer, kind, wanted):
        order = range(pairs) if kind >= 2 else reversed(range(pairs))
        for q in order:
            pl.when(wanted(q))(lambda q=q: far_copy(src, buffer, kind, pair, q).start())

    def far_sent(src, buffer, kind, wanted):
        for q in range(pairs):
            pl.when(wanted(q))(lambda q=q: far_copy(src, buffer, kind, pair, q).wait_send())

    def far_arrived(buffer, kind, place):
        far_copy(buffer.at[place], buffer, kind, place, 0).wait_recv()

    def run(blocks, maps, kind, start, steps, stride):
        running[...] = jnp.zeros_like(running)

        def step(i, carry):
            place = start + stride * i
            far_arrived(blocks, kind, place)

            @pl.when(i > 0)
            def _():
                far_arrived(maps, kind + 1, place)
                matrix = maps[place]
                running[...] = apply_exact(embed(matrix[:w], matrix[w:]), running[...])

            running[...] += blocks[place].astype(F32)
            return carry

        lax.fori_loop(0, steps, step, 0)

    def later_term(q):
        return q > pair

    def later_map(q):
        return jnp.logical_and(pair > 0, q > pair)

    def earlier_term(q):
        return q < pair

    def earlier_map(q):
        return jnp.logical_and(pair < pairs - 1, q < pair)

    def arrived(slot):
        pltpu.make_async_remote_copy(
            src_ref=buffers[slot], dst_ref=buffers[slot], send_sem=send_sem.at[0], recv_sem=recv_sem.at[slot],
            device_id={"slab": s, "row": 1 - r}, device_id_type=pl.DeviceIdType.MESH,
        ).wait_recv()

    def sent(src, out_slot):
        pltpu.make_async_remote_copy(
            src_ref=src, dst_ref=src, send_sem=send_sem.at[out_slot], recv_sem=recv_sem.at[0],
            device_id={"slab": s, "row": 1 - r}, device_id_type=pl.DeviceIdType.MESH,
        ).wait_send()

    barrier = pltpu.get_barrier_semaphore()
    leader = jnp.logical_or(jnp.logical_and(odd == 0, r == 0), jnp.logical_and(odd == 1, r == 1))
    side = jnp.where(r == 1, s + 1, s - 1)
    partners = [
        (s, 1 - r, None),
        (s - 1, r, s > 0),
        (s + 1, r, s < count - 1),
        (side, 1 - r, jnp.logical_and(side >= 0, side < count)),
        (jnp.where(odd == 1, s - 1, s + 1), 1 - r, leader),
    ]
    first_leader = jnp.logical_and(odd == 0, r == 0)
    last_leader = jnp.logical_and(odd == 1, r == 1)
    for q in range(pairs):
        partners.append((2 * q, 0, jnp.logical_and(first_leader, pair != q)))
        partners.append((2 * q + 1, 1, jnp.logical_and(first_leader, q < pair)))
        partners.append((2 * q, 0, jnp.logical_and(last_leader, q > pair)))
    expected = 1
    for slab, row, there in partners:
        def greet(slab=slab, row=row):
            pl.semaphore_signal(
                barrier, inc=1, device_id={"slab": slab, "row": row}, device_id_type=pl.DeviceIdType.MESH
            )
        if there is None:
            greet()
        else:
            pl.when(there)(greet)
            expected = expected + there.astype(jnp.int32)
    pl.semaphore_wait(barrier, expected)

    push(source_hbm, SOURCE, S_SOURCE, s, 1 - r)

    @pl.when(s < count - 1)
    def _():
        push(couple_hbm, COUPLE, S_COUPLE, s + 1, r)

    interior = interior_ref[0]

    def injected(ref, half):
        orbital = half * rows + lax.broadcasted_iota(jnp.int32, (rows, cols), 0)
        live = jnp.logical_or(orbital < w + interior, orbital >= width - w).astype(F32)
        return jnp.concatenate(
            [(ref[0].astype(F32) * live).astype(BF16), (ref[1].astype(F32) * live).astype(BF16)], axis=1
        )

    def add_product(x, columns, first, span=slice(None)):
        by_real = dot(green[0, span, columns], x)
        by_imag = dot(green[1, span, columns], x)
        real = by_real[:, :cols] - by_imag[:, cols:]
        imag = by_real[:, cols:] + by_imag[:, :cols]
        if first:
            out_ref[0], out_ref[1] = real, imag
        else:
            out_ref[0, span, :] += real
            out_ref[1, span, :] += imag

    loads[0].wait()
    loads[1].wait()
    add_product(injected(source, r), pl.ds(pl.multiple_of(r * rows, w), rows), True)
    arrived(SOURCE)

    loads[2].wait()
    head, tail = slice(0, w), slice(width - w, width)
    has_next = (s < count - 1).astype(F32)

    def next_coupling():
        return (couple[...].astype(F32) * has_next).astype(BF16).reshape(2 * w, w)

    def previous_coupling():
        @pl.when(s > 0)
        def _():
            arrived(COUPLE)

        @pl.when(s == 0)
        def _():
            couple_in[...] = jnp.zeros_like(couple_in)

    def previous_adjoint():
        return (
            couple_in[0].astype(F32).T.astype(BF16),
            (-couple_in[1].astype(F32).T).astype(BF16),
        )

    def block(first_row, columns):
        return embed(
            green[0, first_row:first_row + w, columns], green[1, first_row:first_row + w, columns]
        )

    def surface(first_row):
        return jnp.concatenate(
            [out_ref[0, first_row:first_row + w, :], out_ref[1, first_row:first_row + w, :]], axis=0
        )

    def pairwise(ref):
        return jnp.concatenate([ref[:w], ref[w:]], axis=1)

    def no_state(ref, there, slot):
        @pl.when(there)
        def _():
            arrived(slot)

        @pl.when(jnp.logical_not(there))
        def _():
            ref[...] = jnp.zeros_like(ref)

    def row_zero(even):
        there = slice(rows, 2 * rows)
        injection = injected(source_in, 1)
        add_product(injection, there, False, slice(0, w))
        first = surface(0)
        edge_out[...] = first.astype(BF16)

        @pl.when(s > 0)
        def _():
            push(edge_out, EDGE, S_EDGE, s - 1, 1)

        if not even:
            out_0[...] = first
            push(out_0, FIRST_B, S_0, s - 1, 0)
        add_product(injection, there, False, slice(w, rows))
        couple_now = next_coupling()
        back = dot(block(0, tail), couple_now)
        if not even:
            out_1[...] = back
            push(out_1, BACK_B, S_1, s - 1, 0)
        previous_coupling()
        adj_real, adj_imag = previous_adjoint()
        adjoint = embed(adj_real, adj_imag)
        cross = dot(block(0, head), jnp.concatenate([adj_real, adj_imag], axis=0))
        if not even:
            out_2[...] = cross
            push(out_2, CROSS_B, S_2, s - 1, 0)
            couple_map = embed(couple_now[:w], couple_now[w:])
        else:
            couple_map = embed(couple_now[:w], couple_now[w:])
            arrived(BACK_B)
            back_own = wide_map(back)
            ship_map[...] = apply_wide(back_own, back_b[...]).astype(BF16)
            far_push(ship_map, back_maps, 3, earlier_map)
            back_far = wide_map(back_b[...])
            arrived(CROSS_B)
            arrived(MAP_A)
            cross_far = wide_map(cross_b[...])
            cross_two_f = apply_wide(cross_far, map_a[...])
            cross_two = wide_map(cross_two_f)
            cross_all = wide_map(cross + apply_wide(back_own, cross_two_f))
            arrived(FIRST_B)
            arrived(TERM_A)
            term_b = first_b[...] + apply_rounded(cross_far, term_a[...])
            term = first + apply_wide(back_own, term_b)
            run(totals, total_maps, 0, 0, pair, 1)
            before = running[...]
            ship[...] = (term + apply_wide(cross_all, before)).astype(BF16)
            far_push(ship, backs, 2, earlier_term)

            @pl.when(pair > 0)
            def _():
                state[...] = before.astype(BF16)
                push(state, STATE, S_2, s + 1, 1)

            low_out[...] = apply_exact(adjoint, before).astype(BF16)
            push(low_out, LOWER, S_LOWER, s, 1)
            after_own = term_b + apply_wide(cross_two, before)
            add_product(pairwise(low_out), head, False)
            run(backs, back_maps, 2, pairs - 1, pairs - 1 - pair, -1)
            follow = running[...]

            @pl.when(pair < pairs - 1)
            def _():
                after[...] = follow.astype(BF16)
                push(after, AFTER, S_0, s + 1, 0)

            up_out[...] = apply_exact(couple_map, after_own + apply_wide(back_far, follow)).astype(BF16)
            push(up_out, UPPER, S_UPPER, s, 1)
            add_product(pairwise(up_out), tail, False)
            sent(low_out, S_LOWER)
        if not even:
            arrived(LOWER)
            add_product(pairwise(lower), head, False)
            no_state(after, pair < pairs - 1, AFTER)
            up_out[...] = dot(couple_map, after[...]).astype(BF16)
            push(up_out, UPPER, S_UPPER, s, 1)
            add_product(pairwise(up_out), tail, False)
        sent(up_out, S_UPPER)

        @pl.when(s > 0)
        def _():
            sent(edge_out, S_EDGE)

        if even:
            @pl.when(pair > 0)
            def _():
                sent(state, S_2)

            @pl.when(pair < pairs - 1)
            def _():
                sent(after, S_0)

            far_sent(ship_map, back_maps, 3, earlier_map)
            far_sent(ship, backs, 2, earlier_term)
        else:
            sent(out_0, S_0)
            sent(out_1, S_1)
            sent(out_2, S_2)

    def row_one(even):
        add_product(injected(source_in, 0), slice(0, rows), False)
        last = surface(rows - w)
        previous_coupling()
        adj_real, adj_imag = previous_adjoint()
        forward = dot(block(rows - w, head), jnp.concatenate([adj_real, adj_imag], axis=0))
        if even:
            out_0[...] = forward
            push(out_0, MAP_A, S_0, s, 0)
            push(out_0, MAP_A, S_1, s + 1, 1)
        else:
            own = wide_map(forward)
        turned = wide_map(dot(block(rows - w, tail), next_coupling()))
        if even:
            arrived(EDGE)
            edge = edge_in[...]
        else:
            no_state(edge_in, s < count - 1, EDGE)
            edge = edge_in[...]
        term = last + dot(turned[0], edge) + dot(turned[1], edge)
        if even:
            ship[...] = term.astype(BF16)
            push(ship, TERM_A, S_2, s + 1, 1)
            push(ship, TERM_A, S_3, s, 0)
        else:
            arrived(MAP_A)
            ship_map[...] = apply_wide(own, map_a[...]).astype(BF16)
            near = wide_map(map_a[...])
            arrived(TERM_A)
            ship[...] = (term + apply_rounded(own, term_a[...])).astype(BF16)
            far_push(ship, totals, 0, later_term)
            far_push(ship_map, total_maps, 1, later_map)
            no_state(state, pair > 0, STATE)
            before = state[...]
            inner = term_a[...].astype(F32) + apply_rounded(near, before)
            low_out[...] = apply_exact(embed(adj_real, adj_imag), inner).astype(BF16)
            push(low_out, LOWER, S_LOWER, s, 0)
            add_product(pairwise(low_out), head, False)
        if even:
            arrived(LOWER)
            add_product(pairwise(lower), head, False)
        arrived(UPPER)
        add_product(pairwise(upper), tail, False)
        if even:
            sent(out_0, S_0)
            sent(out_0, S_1)
            sent(ship, S_2)
            sent(ship, S_3)
        else:
            far_sent(ship_map, total_maps, 1, later_map)
            far_sent(ship, totals, 0, later_term)
            sent(low_out, S_LOWER)

    for row, role in ((0, row_zero), (1, row_one)):
        for parity in (0, 1):
            @pl.when(jnp.logical_and(r == row, odd == parity))
            def _(role=role, parity=parity):
                role(parity == 0)

    sent(source_hbm, S_SOURCE)

    @pl.when(s < count - 1)
    def _():
        sent(couple_hbm, S_COUPLE)


def body(green_blocks, coupling, source, interior_count):
    rows, width = green_blocks.shape[1:]
    w = coupling.shape[1]
    cols = source.shape[2]
    block = pltpu.VMEM((2 * w, cols), F32)
    small = pltpu.VMEM((2 * w, cols), BF16)
    square = pltpu.VMEM((2 * w, w), F32)
    pairs = lax.axis_size("slab") // 2
    result = pl.pallas_call(
        functools.partial(kernel, lax.axis_size("slab")),
        out_shape=pltpu.VMEM((2, rows, cols), F32),
        in_specs=[pl.BlockSpec(memory_space=pltpu.HBM)] * 3 + [pl.BlockSpec(memory_space=pltpu.SMEM)],
        out_specs=pl.BlockSpec(memory_space=pltpu.VMEM),
        scratch_shapes=[
            pltpu.VMEM(green_blocks.shape, BF16),
            pltpu.VMEM(coupling.shape, BF16),
            pltpu.VMEM(source.shape, BF16),
            pltpu.VMEM(source.shape, BF16),
            pltpu.VMEM(coupling.shape, BF16),
            small,
            square,
            small,
            square,
            square,
            block,
            small,
            small,
            small,
            small,
            small,
            block,
            block,
            square,
            small,
            small,
            small,
            pltpu.VMEM((pairs, 2 * w, cols), BF16),
            pltpu.VMEM((pairs, 2 * w, w), BF16),
            pltpu.VMEM((pairs, 2 * w, cols), BF16),
            pltpu.VMEM((pairs, 2 * w, w), BF16),
            pltpu.VMEM((2 * w, w), BF16),
            block,
            pltpu.SemaphoreType.DMA((3,)),
            pltpu.SemaphoreType.DMA((9,)),
            pltpu.SemaphoreType.DMA((12,)),
            pltpu.SemaphoreType.DMA((2, pairs)),
            pltpu.SemaphoreType.DMA((4, pairs)),
        ],
        compiler_params=pltpu.CompilerParams(
            collective_id=0, has_side_effects=True, vmem_limit_bytes=60 * 1024 * 1024
        ),
    )(green_blocks, coupling, source, interior_count)
    orbital = lax.axis_index("row") * rows + lax.iota(jnp.int32, rows)
    live = ((orbital < w + interior_count[0]) | (orbital >= width - w)).astype(F32)
    return result * live[None, :, None]


def solution(mesh):
    placed = (
        P(None, ("energy", "slab", "row"), None),
        P(None, "slab", None),
        P(None, ("energy", "slab", "row"), None),
        P("slab"),
    )
    return jax.shard_map(
        body,
        mesh=mesh,
        in_specs=placed,
        out_specs=P(None, ("energy", "slab", "row"), None),
        check_vma=False,
    )
```
